128 devices in a mesh: dp: 8 (over x, z_hi), vocab: 16 (over z_lo, y, core).
Axes of the slice: x: 4, y: 4, z: 4 (z_hi: 2, z_lo: 2; z = z_hi * 2 + z_lo), core: 2. Of those that a mesh axis runs over, the one named last changes fastest.
Arguments:
- query_hidden: bfloat16 [16, 128, 4096], P('dp', None, 'vocab'), may hold values from -144 to 144
- passage_hidden: bfloat16 [16, 256, 4096], P('dp', None, 'vocab'), may hold values from -144 to 144
- head_weight: bfloat16 [4096, 32768], P(None, 'vocab'), may hold values from -6 to 6
- query_mask: int32 [16, 128], P('dp'), may hold values from 0 to 1, as said below
- passage_mask: int32 [16, 256], P('dp'), may hold values from 0 to 1, as said below
- positive: int32 [16], replicated, may hold values from 0 to 15
Outputs:
- grad_query_hidden: bfloat16 [16, 128, 4096], P('dp', None, 'vocab')
- grad_passage_hidden: bfloat16 [16, 256, 4096], P('dp', None, 'vocab')
- query_loss: float32 [16], P('dp')
The draws below stay inside these ranges and needn't reach their ends.
Inputs may be any that keep to these rules, and one draw needn't show every extreme that they name: `query_mask`: the live tokens of each query are a prefix of 32 to 128 positions. `passage_mask`: the live tokens of each passage are a prefix of 64 to 256 positions.
All inputs are finite; a program needn't handle non-finite values.
Results may differ from the reference program's by a relative error of at most 0.0095.
Values may be sent and summed in bfloat16 or wider, within the bound.
No kernel may reach another device: no remote copies, remote signals or barrier semaphores. Data moves between devices by JAX's collectives and lax.ppermute only.
A program may use at most 128 MiB of HBM per device.

```python
import math
import jax
import jax.numpy as jnp
from jax import lax

D = 4096
QLEN = 128
PLEN = 256
VOCAB = 32768
QUERIES = 16
PASSAGES = 16


def hidden_states(key, count, length):
    values = jnp.clip(jax.random.normal(key, (count, length, D), jnp.float32), -6.0, 6.0)
    return values.astype(jnp.bfloat16)


def prefix_mask(key, count, length):
    lengths = jax.random.randint(key, (count,), length // 4, length + 1)
    return (jnp.arange(length, dtype=jnp.int32)[None, :] < lengths[:, None]).astype(jnp.int32)


def draw_query_hidden(key, part):
    return hidden_states(jax.random.fold_in(key, 11), QUERIES, QLEN)


def draw_passage_hidden(key, part):
    return hidden_states(jax.random.fold_in(key, 13), PASSAGES, PLEN)


def draw_head_weight(key, part):
    inner = jax.random.fold_in(key, 23)
    column = jnp.arange(VOCAB, dtype=jnp.float32) / (VOCAB - 1.0)
    values = jnp.clip(jax.random.normal(inner, (D, VOCAB), jnp.float32), -6.0, 6.0)
    ramp = jnp.exp(math.log(0.4) + math.log(10.0) * column)
    return (values * ramp[None, :] / math.sqrt(D)).astype(jnp.bfloat16)


def draw_query_mask(key, part):
    return prefix_mask(jax.random.fold_in(key, 17), QUERIES, QLEN)


def draw_passage_mask(key, part):
    return prefix_mask(jax.random.fold_in(key, 19), PASSAGES, PLEN)


def with_ends(array, rng, least, largest):
    index_at = [jax.random.randint(jax.random.fold_in(rng, axis), (), 0, length) for axis, length in enumerate(array.shape)]
    longest = array.shape.index(max(array.shape))
    neighbour = index_at[:longest] + [(index_at[longest] + 1) % array.shape[longest]] + index_at[longest + 1:]
    return array.at[tuple(index_at)].set(least).at[tuple(neighbour)].set(largest)


def setup_inputs(seed: int = 0) -> dict:
    arg_keys = jax.random.split(jax.random.key(seed), 7)
    return {
        "query_hidden": draw_query_hidden(jax.random.fold_in(arg_keys[6], 71), 0),
        "passage_hidden": draw_passage_hidden(jax.random.fold_in(arg_keys[6], 71), 0),
        "head_weight": draw_head_weight(jax.random.fold_in(arg_keys[6], 71), 0),
        "query_mask": draw_query_mask(jax.random.fold_in(arg_keys[6], 71), 0),
        "passage_mask": draw_passage_mask(jax.random.fold_in(arg_keys[6], 71), 0),
        "positive": with_ends(jax.random.randint(arg_keys[5], (QUERIES,), 0, PASSAGES), jax.random.fold_in(arg_keys[5], 1), 0, PASSAGES - 1).astype(jnp.int32),
    }


normalizer_sharpness = 0.2
score_div = 16.0
loss_scale = 65536.0


def pool_seq(lexicon_projection_lines, live):
    divided_similarity_matrix = lexicon_projection_lines / normalizer_sharpness
    live_rows = live[:, None] > 0
    largest_element = jnp.max(jnp.where(live_rows, divided_similarity_matrix, -1e30), axis=0)
    expo = jnp.where(live_rows, jnp.exp(divided_similarity_matrix - largest_element[None, :]), 0.0)
    cumulative_accumulator = jnp.sum(expo, axis=0)
    softened_rectifier_output = normalizer_sharpness * (largest_element + jnp.log(cumulative_accumulator))
    return softened_rectifier_output, expo / cumulative_accumulator[None, :]


def forward_pool(hidden, mask, head_weight):
    def single(args):
        rows, live = args
        lexicon_projection_lines = jnp.dot(rows, head_weight, preferred_element_type=jnp.float32)
        softened_rectifier_output, share = pool_seq(lexicon_projection_lines, live)
        return softened_rectifier_output
    return lax.map(single, (hidden, mask))


def reverse_max_reduce(hidden, mask, head_weight, dpooled):
    def single(args):
        rows, live, dpool = args
        lexicon_projection_lines = jnp.dot(rows, head_weight, preferred_element_type=jnp.float32)
        softened_rectifier_output, share = pool_seq(lexicon_projection_lines, live)
        dsmooth = dpool * jnp.where(softened_rectifier_output > 0, 1.0 / (1.0 + jnp.maximum(softened_rectifier_output, 0.0)), 0.0)
        dlogits = (share * dsmooth[None, :]).astype(jnp.bfloat16)
        return jnp.dot(dlogits, head_weight.T, preferred_element_type=jnp.float32).astype(jnp.bfloat16)
    return lax.map(single, (hidden, mask, dpooled))


def reference(query_hidden, passage_hidden, head_weight, query_mask, passage_mask, positive):
    q_smooth = forward_pool(query_hidden, query_mask, head_weight)
    p_smooth = forward_pool(passage_hidden, passage_mask, head_weight)
    q_pooled = jnp.log1p(jnp.maximum(q_smooth, 0.0))
    p_pooled = jnp.log1p(jnp.maximum(p_smooth, 0.0))
    scores = jnp.dot(q_pooled, p_pooled.T, precision=lax.Precision.HIGHEST, preferred_element_type=jnp.float32) / score_div
    largest_element = jnp.max(scores, axis=1)
    lse = largest_element + jnp.log(jnp.sum(jnp.exp(scores - largest_element[:, None]), axis=1))
    picked = (positive[:, None] == jnp.arange(PASSAGES, dtype=jnp.int32)[None, :]).astype(jnp.float32)
    query_loss = lse - jnp.sum(scores * picked, axis=1)
    probs = jnp.exp(scores - lse[:, None])
    dscores = (probs - picked) * (loss_scale / QUERIES)
    dq_pooled = jnp.dot(dscores, p_pooled, precision=lax.Precision.HIGHEST, preferred_element_type=jnp.float32) / score_div
    grad_passage_summary = jnp.dot(dscores.T, q_pooled, precision=lax.Precision.HIGHEST, preferred_element_type=jnp.float32) / score_div
    grad_query_hidden = reverse_max_reduce(query_hidden, query_mask, head_weight, dq_pooled)
    grad_passage_hidden = reverse_max_reduce(passage_hidden, passage_mask, head_weight, grad_passage_summary)
    return grad_query_hidden, grad_passage_hidden, query_loss
```

```python
import functools

import jax
import jax.numpy as jnp
from jax import lax
from jax.experimental import pallas as pl
from jax.experimental.pallas import tpu as pltpu
from jax.sharding import PartitionSpec as P

SHARP = 0.2
DIV = 16.0
LOSS_SCALE = 65536.0
BF = jnp.bfloat16
F32 = jnp.float32
VLIM = 56 * 1024 * 1024
BLK = 256


def y_perm(k):
    return [(z * 8 + y * 2 + c, z * 8 + ((y + k) % 4) * 2 + c) for z in range(2) for y in range(4) for c in range(2)]


Z_SWAP = [(v, v ^ 8) for v in range(16)]
CORE_SWAP = [(v, v ^ 1) for v in range(16)]


def to_y(x, k):
    return lax.ppermute(x, "vocab", y_perm(k % 4))


def to_z(x):
    return lax.ppermute(x, "vocab", Z_SWAP)


def to_core(x):
    return lax.ppermute(x, "vocab", CORE_SWAP)


def to_x(x, k):
    return lax.ppermute(x, "dp", [(g, ((g // 2 + k) % 4) * 2 + g % 2) for g in range(8)])


def to_zhi(x):
    return lax.ppermute(x, "dp", [(g, g ^ 1) for g in range(8)])


def load_operands(copies, nk, bn, steps, idx, xrefs, w, xs, ws, xsem, wsem):
    j = pl.program_id(0)

    def x_copy(i):
        a, k, src, dst, n = copies[i]
        return pltpu.make_async_copy(
            xrefs[a].at[pl.ds(src, n), :], xs.at[pl.ds(dst, n), pl.ds(k * BLK, BLK)], xsem.at[i]
        )

    def w_copy(step, slot, k):
        row = pl.multiple_of(idx[k] * BLK, BLK)
        col = pl.multiple_of(step * bn, bn)
        return pltpu.make_async_copy(
            w.at[pl.ds(row, BLK), pl.ds(col, bn)], ws.at[slot, pl.ds(k * BLK, BLK), :], wsem.at[slot, k]
        )

    slot = lax.rem(j, 2)

    @pl.when(j == 0)
    def _():
        for k in range(nk):
            w_copy(0, 0, k).start()
        for i in range(len(copies)):
            x_copy(i).start()

    @pl.when(j + 1 < steps)
    def _():
        for k in range(nk):
            w_copy(j + 1, 1 - slot, k).start()

    @pl.when(j == 0)
    def _():
        for i in range(len(copies)):
            x_copy(i).wait()

    for k in range(nk):
        w_copy(j, slot, k).wait()
    return slot


def logits_kernel(copies, nk, nx, bn, steps, has_acc, idx, *refs):
    xrefs = refs[:nx]
    w = refs[nx]
    pos = nx + 1
    acc = None
    if has_acc:
        acc = refs[pos]
        pos += 1
    out, xs, ws, xsem, wsem = refs[pos:]
    slot = load_operands(copies, nk, bn, steps, idx, xrefs, w, xs, ws, xsem, wsem)
    res = jnp.dot(xs[...], ws[slot], preferred_element_type=F32)
    if has_acc:
        res = res + acc[...]
    out[...] = res


def logits_part(arrays, copies, idx, w, acc):
    rows = 768
    cols = w.shape[1]
    nk = idx.shape[0]
    bn = 512
    steps = cols // bn
    any_spec = pl.BlockSpec(memory_space=pl.ANY)
    blk = pl.BlockSpec((rows, bn), lambda j, *_: (0, j))
    ins = list(arrays) + [w] + ([acc] if acc is not None else [])
    return pl.pallas_call(
        functools.partial(logits_kernel, copies, nk, len(arrays), bn, steps, acc is not None),
        grid_spec=pltpu.PrefetchScalarGridSpec(
            num_scalar_prefetch=1,
            grid=(steps,),
            in_specs=[any_spec] * (len(arrays) + 1) + ([blk] if acc is not None else []),
            out_specs=blk,
            scratch_shapes=[
                pltpu.VMEM((rows, nk * BLK), BF),
                pltpu.VMEM((2, nk * BLK, bn), BF),
                pltpu.SemaphoreType.DMA((len(copies),)),
                pltpu.SemaphoreType.DMA((2, nk)),
            ],
        ),
        out_shape=jax.ShapeDtypeStruct((rows, cols), F32),
        compiler_params=pltpu.CompilerParams(vmem_limit_bytes=VLIM),
        name="logits_part",
    )(idx, *ins)


def pool_kernel(copies, nk, nx, bn, steps, seqs, idx, lens, *refs):
    xrefs = refs[:nx]
    w, acc, expo, stats, xs, ws, xsem, wsem = refs[nx:]
    slot = load_operands(copies, nk, bn, steps, idx, xrefs, w, xs, ws, xsem, wsem)
    logits = jnp.dot(xs[...], ws[slot], preferred_element_type=F32) + acc[...]
    smooth, sums = [], []
    for s, (start, n) in enumerate(seqs):
        part = logits[start : start + n] * (1.0 / SHARP)
        live = lax.broadcasted_iota(jnp.int32, (n, 1), 0) < lens[s]
        top = jnp.max(jnp.where(live, part, -1e30), axis=0, keepdims=True)
        e = jnp.where(live, jnp.exp(part - top), 0.0)
        total = jnp.sum(e, axis=0, keepdims=True)
        expo[pl.ds(start, n), :] = e
        smooth.append(SHARP * (top + jnp.log(total)))
        sums.append(total)
    stats[...] = jnp.concatenate(smooth + sums, axis=0)


def logits_pool(arrays, copies, idx, lens, w, acc, seqs):
    rows = 768
    cols = w.shape[1]
    nk = idx.shape[0]
    bn = 512
    steps = cols // bn
    any_spec = pl.BlockSpec(memory_space=pl.ANY)
    blk = pl.BlockSpec((rows, bn), lambda j, *_: (0, j))
    return pl.pallas_call(
        functools.partial(pool_kernel, copies, nk, len(arrays), bn, steps, seqs),
        grid_spec=pltpu.PrefetchScalarGridSpec(
            num_scalar_prefetch=2,
            grid=(steps,),
            in_specs=[any_spec] * (len(arrays) + 1) + [blk],
            out_specs=[blk, pl.BlockSpec((8, bn), lambda j, *_: (0, j))],
            scratch_shapes=[
                pltpu.VMEM((rows, nk * BLK), BF),
                pltpu.VMEM((2, nk * BLK, bn), BF),
                pltpu.SemaphoreType.DMA((len(copies),)),
                pltpu.SemaphoreType.DMA((2, nk)),
            ],
        ),
        out_shape=[jax.ShapeDtypeStruct((rows, cols), F32), jax.ShapeDtypeStruct((8, cols), F32)],
        compiler_params=pltpu.CompilerParams(vmem_limit_bytes=VLIM),
        name="logits_pool",
    )(idx, lens, *arrays, w, acc)


def exact_dot(a, b, dims):
    return lax.dot_general(a, b, (dims, ((), ())), precision=lax.Precision.HIGHEST, preferred_element_type=F32)


def gram_kernel(a, b, out):
    every = jnp.concatenate([a[...], b[...]], axis=0)
    out[...] = exact_dot(every, every, ((1,), (1,)))


def gram(a, b):
    n = a.shape[0] + b.shape[0]
    return pl.pallas_call(
        gram_kernel,
        out_shape=jax.ShapeDtypeStruct((n, n), F32),
        compiler_params=pltpu.CompilerParams(vmem_limit_bytes=VLIM),
        name="gram",
    )(a, b)


def nt_dot(a, b):
    return lax.dot_general(a, b, (((1,), (1,)), ((), ())), preferred_element_type=F32)


def first_grad_kernel(seqs, nk, total_queries, idx, parts, pa, pb, stats, picked, expo, w, dl, loss, *refs):
    outs = refs[:nk]
    es, ws, esem, wsem = refs[nk:]

    def e_copy(s):
        start, n = seqs[s]
        return pltpu.make_async_copy(expo.at[pl.ds(start, n), :], es.at[pl.ds(start, n), :], esem.at[s])

    def w_copy(k):
        row = pl.multiple_of(idx[k] * BLK, BLK)
        return pltpu.make_async_copy(w.at[pl.ds(row, BLK), :], ws.at[k], wsem.at[k])

    for s in range(len(seqs)):
        e_copy(s).start()
    for k in range(nk):
        w_copy(k).start()

    scores = parts[0]
    for i in range(1, parts.shape[0]):
        scores = scores + parts[i]
    scores = scores / DIV
    n = scores.shape[0]
    row = lax.broadcasted_iota(jnp.int32, (n, n), 0)
    col = lax.broadcasted_iota(jnp.int32, (n, n), 1)
    is_q = (row % 4) < 2
    is_p = (col % 4) >= 2
    masked = jnp.where(is_p, scores, -1e30)
    top = jnp.max(masked, axis=1, keepdims=True)
    lse = top + jnp.log(jnp.sum(jnp.where(is_p, jnp.exp(masked - top), 0.0), axis=1, keepdims=True))
    pick = picked[...]
    losses = lse - jnp.sum(scores * pick, axis=1, keepdims=True)
    loss[...] = jnp.broadcast_to(losses[:8], loss.shape)
    probs = jnp.where(is_p, jnp.exp(masked - lse), 0.0)
    dscores = jnp.where(is_q, (probs - pick) * (LOSS_SCALE / total_queries), 0.0)
    both = dscores + dscores.T
    every = jnp.concatenate([pa[...], pb[...]], axis=0)
    dpooled = exact_dot(both[:8], every, ((1,), (0,))) / DIV
    smooth = stats[0:4, :]
    gate = jnp.where(smooth > 0, 1.0 / (1.0 + jnp.maximum(smooth, 0.0)), 0.0)
    g = dpooled[:4] * gate / stats[4:8, :]
    for s, (start, n) in enumerate(seqs):
        e_copy(s).wait()
        dl[pl.ds(start, n), :] = (es[pl.ds(start, n), :] * g[s : s + 1, :]).astype(BF)
    for k in range(nk):
        w_copy(k).wait()
        outs[k][...] = nt_dot(dl[...], ws[k]).astype(outs[k].dtype)


def first_grad(idx, parts, pa, pb, stats, picked, expo, w, seqs, dtypes, total_queries):
    rows, cols = expo.shape
    nk = len(dtypes)
    vm = pl.BlockSpec(memory_space=pltpu.VMEM)
    any_spec = pl.BlockSpec(memory_space=pl.ANY)
    return pl.pallas_call(
        functools.partial(first_grad_kernel, seqs, nk, total_queries),
        in_specs=[pl.BlockSpec(memory_space=pltpu.SMEM)] + [vm] * 5 + [any_spec] * 2,
        out_specs=[vm] * (2 + nk),
        scratch_shapes=[
            pltpu.VMEM((rows, cols), F32),
            pltpu.VMEM((nk, BLK, cols), BF),
            pltpu.SemaphoreType.DMA((len(seqs),)),
            pltpu.SemaphoreType.DMA((nk,)),
        ],
        out_shape=[jax.ShapeDtypeStruct((rows, cols), BF), jax.ShapeDtypeStruct((8, 128), F32)]
        + [jax.ShapeDtypeStruct((rows, BLK), t) for t in dtypes],
        compiler_params=pltpu.CompilerParams(vmem_limit_bytes=VLIM),
        name="first_grad",
    )(idx, parts, pa, pb, stats, picked, expo, w)


def grad_kernel(nk, idx, dl, w, *refs):
    outs = refs[:nk]
    ws, wsem = refs[nk:]

    def w_copy(k):
        row = pl.multiple_of(idx[k] * BLK, BLK)
        return pltpu.make_async_copy(w.at[pl.ds(row, BLK), :], ws.at[k], wsem.at[k])

    for k in range(nk):
        w_copy(k).start()
    for k in range(nk):
        w_copy(k).wait()
        outs[k][...] = nt_dot(dl[...], ws[k]).astype(outs[k].dtype)


def grad_part(idx, dl, w, dtypes):
    rows, cols = dl.shape
    nk = len(dtypes)
    vm = pl.BlockSpec(memory_space=pltpu.VMEM)
    return pl.pallas_call(
        functools.partial(grad_kernel, nk),
        in_specs=[pl.BlockSpec(memory_space=pltpu.SMEM), vm, pl.BlockSpec(memory_space=pl.ANY)],
        out_specs=[vm] * nk,
        scratch_shapes=[pltpu.VMEM((nk, BLK, cols), BF), pltpu.SemaphoreType.DMA((nk,))],
        out_shape=[jax.ShapeDtypeStruct((rows, BLK), t) for t in dtypes],
        compiler_params=pltpu.CompilerParams(vmem_limit_bytes=VLIM),
        name="grad_part",
    )(idx, dl, w)


def on_device(query_hidden, passage_hidden, head_weight, query_mask, passage_mask, positive):
    q_count, q_len, width = query_hidden.shape
    p_count, p_len, _ = passage_hidden.shape
    w = head_weight
    split = q_count * q_len
    seqs = tuple((i * q_len, q_len) for i in range(q_count)) + tuple(
        (split + i * p_len, p_len) for i in range(p_count)
    )
    own = jnp.concatenate([query_hidden.reshape(split, width), passage_hidden.reshape(p_count * p_len, width)], axis=0)

    vocab = lax.axis_index("vocab")
    z, y, core = vocab // 8, (vocab // 2) % 4, vocab % 2

    def block(dy, dz):
        base = ((z + dz) % 2) * 8 + ((y + dy) % 4) * 2
        return [base + core, base + 1 - core]

    def index(*places):
        return jnp.stack([b for p in places for b in block(*p)]).astype(jnp.int32)

    x10, xm0, x01 = to_y(own, -1), to_y(own, 1), to_z(own)
    own_s = to_core(own)
    h = 384
    f1 = to_y(jnp.concatenate([x10[:h], x01[h:]], axis=0), -1)
    f2 = to_y(jnp.concatenate([x01[h:], xm0[h:]], axis=0), 1)
    f3 = to_z(jnp.concatenate([x10[:h], xm0[:h]], axis=0))
    near = [own, own_s] + [t for p in (x10, xm0, x01) for t in (p, to_core(p))]
    whole = tuple((i, i, 0, 0, 768) for i in range(8))
    acc = logits_part(near, whole, index((0, 0), (1, 0), (-1, 0), (0, 1)), w, None)
    g1 = to_y(f3[:256], -1)
    g2 = to_z(jnp.concatenate([f1[256:384], f2[384:512]], axis=0))
    g3 = to_y(f2[128:384], 1)
    mid = [t for p in (f1, f2, f3) for t in (p, to_core(p))]
    mid_copies = []
    for c in range(2):
        mid_copies += [
            (0 + c, 0 + c, 0, 0, h),
            (2 + c, 0 + c, h, h, h),
            (4 + c, 2 + c, 0, 0, h),
            (0 + c, 2 + c, h, h, h),
            (4 + c, 4 + c, h, 0, h),
            (2 + c, 4 + c, 0, h, h),
        ]
    acc = logits_part(mid, tuple(mid_copies), index((2, 0), (1, 1), (-1, 1)), w, acc)
    last = [t for p in (g1, g2, g3) for t in (p, to_core(p))]
    last_copies = tuple((2 * i + c, c, 0, 256 * i, 256) for i in range(3) for c in range(2))
    lens = jnp.concatenate([jnp.sum(query_mask > 0, axis=1), jnp.sum(passage_mask > 0, axis=1)]).astype(jnp.int32)
    expo, stats = logits_pool(last, last_copies, index((2, 1)), lens, w, acc, seqs)

    pooled = jnp.log1p(jnp.maximum(stats[:4], 0.0))
    pa = jnp.concatenate([pooled] + [to_x(pooled, -k) for k in (1, 2, 3)], axis=0)
    pb = to_zhi(pa)
    part = gram(pa, pb)
    parts = lax.all_to_all(jnp.broadcast_to(part, (16,) + part.shape), "vocab", 0, 0)

    group = lax.axis_index("dp")
    slot = jnp.arange(32, dtype=jnp.int32)
    place = slot // 4
    gx = (group // 2 + place % 4) % 4
    gz = (group % 2 + place // 4) % 2
    seq = (gx * 2 + gz) * 2 + slot % 2
    target = positive[seq]
    picked = ((target[:, None] == seq[None, :]) & (slot[:, None] % 4 < 2) & (slot[None, :] % 4 >= 2)).astype(F32)

    dl, loss, m21, s21 = first_grad(
        index((2, 1)), parts, pa, pb, stats, picked, expo, w, seqs, (F32, BF), positive.shape[0]
    )
    t21 = (m21 + to_core(s21)).astype(BF)
    r1, r2, r3 = to_y(t21[:256], 1), to_z(t21[256:512]), to_y(t21[512:], -1)
    m20, s20, m11, s11, mm1, sm1 = grad_part(index((2, 0), (1, 1), (-1, 1)), dl, w, (F32, BF) * 3)

    def pad(part, start):
        return jnp.pad(part.astype(F32), ((start, 768 - start - part.shape[0]), (0, 0)))

    t20 = (m20 + to_core(s20) + pad(r2, 256)).astype(BF)
    t11 = (m11 + to_core(s11) + pad(r1, 0)).astype(BF)
    tm1 = (mm1 + to_core(sm1) + pad(r3, 512)).astype(BF)
    u1 = to_y(jnp.concatenate([t20[:h], t11[h:]], axis=0), 1)
    u2 = to_y(jnp.concatenate([tm1[h:], t20[h:]], axis=0), -1)
    u3 = to_z(jnp.concatenate([t11[:h], tm1[:h]], axis=0))
    m10, s10, mm0, sm0, m01, s01, m00, s00 = grad_part(index((1, 0), (-1, 0), (0, 1), (0, 0)), dl, w, (F32, BF) * 4)
    t10 = (m10 + to_core(s10) + pad(u1[:h], 0) + pad(u3[:h], 0)).astype(BF)
    tm0 = (mm0 + to_core(sm0) + pad(u3[h:], 0) + pad(u2[h:], h)).astype(BF)
    t01 = (m01 + to_core(s01) + pad(u1[h:], h) + pad(u2[:h], h)).astype(BF)
    v1, v2, v3 = to_y(t10, 1), to_y(tm0, -1), to_z(t01)
    out = m00 + to_core(s00) + v1.astype(F32) + v2.astype(F32) + v3.astype(F32)
    out = out.astype(BF)
    return (
        out[:split].reshape(q_count, q_len, width),
        out[split:].reshape(p_count, p_len, width),
        loss[:q_count, 0],
    )


def solution(mesh):
    return jax.shard_map(
        on_device,
        mesh=mesh,
        in_specs=(
            P("dp", None, "vocab"),
            P("dp", None, "vocab"),
            P(None, "vocab"),
            P("dp", None),
            P("dp", None),
            P(),
        ),
        out_specs=(P("dp", None, "vocab"), P("dp", None, "vocab"), P("dp")),
        check_vma=False,
    )
```

```python
import functools

import jax
import jax.numpy as jnp
import numpy as np
from jax import lax
from jax.experimental import pallas as pl
from jax.experimental.pallas import tpu as pltpu
from jax.sharding import PartitionSpec as P

SHARP = 0.2
DIV = 16.0
LOSS_SCALE = 65536.0
BF = jnp.bfloat16
F32 = jnp.float32
MIB = 1024 * 1024
BLK = 256
HBM_SPEC = pl.BlockSpec(memory_space=pltpu.HBM)


def y_perm(k):
    return [(z * 8 + y * 2 + c, z * 8 + ((y + k) % 4) * 2 + c) for z in range(2) for y in range(4) for c in range(2)]


Z_SWAP = [(v, v ^ 8) for v in range(16)]
CORE_SWAP = [(v, v ^ 1) for v in range(16)]


def to_y(x, k):
    return lax.ppermute(x, "vocab", y_perm(k % 4))


def to_z(x):
    return lax.ppermute(x, "vocab", Z_SWAP)


def to_core(x):
    return lax.ppermute(x, "vocab", CORE_SWAP)


def to_x(x, k):
    return lax.ppermute(x, "dp", [(g, ((g // 2 + k) % 4) * 2 + g % 2) for g in range(8)])


def to_zhi(x):
    return lax.ppermute(x, "dp", [(g, g ^ 1) for g in range(8)])


PLACES = ((0, 0), (1, 0), (-1, 0), (0, 1), (2, 0), (1, 1), (-1, 1), (2, 1))


def place_table():
    rows = []
    for v in range(16):
        z, y, core = v // 8, (v // 2) % 4, v % 2
        rows.append([((z + dz) % 2) * 4 + (y + dy) % 4 for dy, dz in PLACES] + [core] * 8)
    return np.array(rows, np.int32)


def matmul_cost(m, k, n):
    return pl.CostEstimate(flops=2 * m * k * n, bytes_accessed=2 * k * n, transcendentals=0)


def load_operands(copies, places, bn, steps, idx, xrefs, w, xs, ws, xsem, wsem):
    j = pl.program_id(0)
    nk = 2 * len(places)

    def x_copy(i):
        a, k, src, dst, n = copies[i]
        return pltpu.make_async_copy(
            xrefs[a].at[pl.ds(src, n), :], xs.at[pl.ds(dst, n), pl.ds(k * BLK, BLK)], xsem.at[i]
        )

    def w_copy(step, slot, k):
        core = idx[8]
        side = core if k % 2 == 0 else 1 - core
        row = pl.multiple_of((idx[places[k // 2]] * 2 + side) * BLK, BLK)
        col = pl.multiple_of(step * bn, bn)
        return pltpu.make_async_copy(
            w.at[pl.ds(row, BLK), pl.ds(col, bn)], ws.at[slot, pl.ds(k * BLK, BLK), :], wsem.at[slot, k]
        )

    slot = lax.rem(j, 2)

    @pl.when(j == 0)
    def _():
        for k in range(nk):
            w_copy(0, 0, k).start()
        for i in range(len(copies)):
            x_copy(i).start()

    @pl.when(j + 1 < steps)
    def _():
        for k in range(nk):
            w_copy(j + 1, 1 - slot, k).start()

    @pl.when(j == 0)
    def _():
        for i in range(len(copies)):
            x_copy(i).wait()

    for k in range(nk):
        w_copy(j, slot, k).wait()
    return slot


def logits_kernel(copies, places, nx, bn, steps, has_acc, idx, *refs):
    xrefs = refs[:nx]
    w = refs[nx]
    pos = nx + 1
    acc = None
    if has_acc:
        acc = refs[pos]
        pos += 1
    out, xs, ws, xsem, wsem = refs[pos:]
    slot = load_operands(copies, places, bn, steps, idx, xrefs, w, xs, ws, xsem, wsem)
    res = jnp.dot(xs[...], ws[slot], preferred_element_type=F32)
    if has_acc:
        res = res + acc[...]
    out[...] = res


def logits_part(arrays, copies, places, idx, w, acc, out_space=None):
    rows = 768
    cols = w.shape[1]
    nk = 2 * len(places)
    bn = 512
    steps = cols // bn
    any_spec = pl.BlockSpec(memory_space=pl.ANY)
    blk = pl.BlockSpec((rows, bn), lambda j, *_: (0, j))
    ins = list(arrays) + [w] + ([acc] if acc is not None else [])
    return pl.pallas_call(
        functools.partial(logits_kernel, copies, places, len(arrays), bn, steps, acc is not None),
        grid_spec=pltpu.PrefetchScalarGridSpec(
            num_scalar_prefetch=1,
            grid=(steps,),
            in_specs=[any_spec] * len(arrays) + [HBM_SPEC] + ([blk] if acc is not None else []),
            out_specs=blk,
            scratch_shapes=[
                pltpu.VMEM((rows, nk * BLK), BF),
                pltpu.VMEM((2, nk * BLK, bn), BF),
                pltpu.SemaphoreType.DMA((len(copies),)),
                pltpu.SemaphoreType.DMA((2, nk)),
            ],
        ),
        out_shape=jax.ShapeDtypeStruct((rows, cols), F32) if out_space is None else out_space((rows, cols), F32),
        compiler_params=pltpu.CompilerParams(vmem_limit_bytes=18 * MIB),
        name="logits_part",
        cost_estimate=matmul_cost(rows, nk * BLK, cols),
    )(idx, *ins)


def pool_kernel(copies, places, nx, bn, steps, seqs, idx, lens, *refs):
    xrefs = refs[:nx]
    w, acc, expo, stats, pooled, xs, ws, xsem, wsem = refs[nx:]
    slot = load_operands(copies, places, bn, steps, idx, xrefs, w, xs, ws, xsem, wsem)
    logits = jnp.dot(xs[...], ws[slot], preferred_element_type=F32) + acc[...]
    smooth, sums = [], []
    for s, (start, n) in enumerate(seqs):
        part = logits[start : start + n] * (1.0 / SHARP)
        live = lax.broadcasted_iota(jnp.int32, (n, 1), 0) < lens[s]
        part = jnp.where(live, part, -1e30)
        top = jnp.max(part, axis=0, keepdims=True)
        e = jnp.exp(part - top)
        total = jnp.sum(e, axis=0, keepdims=True)
        expo[pl.ds(start, n), :] = e.astype(BF)
        smooth.append(SHARP * (top + jnp.log(total)))
        sums.append(total)
    both = jnp.concatenate(smooth + sums, axis=0)
    stats[...] = both
    pooled[...] = jnp.log1p(jnp.maximum(both[:4], 0.0))


def logits_pool(arrays, copies, places, idx, lens, w, acc, seqs):
    rows = 768
    cols = w.shape[1]
    nk = 2 * len(places)
    bn = 512
    steps = cols // bn
    any_spec = pl.BlockSpec(memory_space=pl.ANY)
    blk = pl.BlockSpec((rows, bn), lambda j, *_: (0, j))
    return pl.pallas_call(
        functools.partial(pool_kernel, copies, places, len(arrays), bn, steps, seqs),
        grid_spec=pltpu.PrefetchScalarGridSpec(
            num_scalar_prefetch=2,
            grid=(steps,),
            in_specs=[any_spec] * len(arrays) + [HBM_SPEC, blk],
            out_specs=[
                blk,
                pl.BlockSpec((8, bn), lambda j, *_: (0, j)),
                pl.BlockSpec((4, bn), lambda j, *_: (0, j)),
            ],
            scratch_shapes=[
                pltpu.VMEM((rows, nk * BLK), BF),
                pltpu.VMEM((2, nk * BLK, bn), BF),
                pltpu.SemaphoreType.DMA((len(copies),)),
                pltpu.SemaphoreType.DMA((2, nk)),
            ],
        ),
        out_shape=[
            pltpu.HBM((rows, cols), BF),
            jax.ShapeDtypeStruct((8, cols), F32),
            jax.ShapeDtypeStruct((4, cols), F32),
        ],
        compiler_params=pltpu.CompilerParams(vmem_limit_bytes=20 * MIB),
        name="logits_pool",
        cost_estimate=matmul_cost(rows, nk * BLK, cols),
    )(idx, lens, *arrays, w, acc)


def exact_dot(a, b, dims):
    return lax.dot_general(a, b, (dims, ((), ())), precision=lax.Precision.HIGHEST, preferred_element_type=F32)


def split_kinds(a, b):
    every = jnp.concatenate([a, b], axis=0)
    q = jnp.concatenate([every[i : i + 2] for i in range(0, every.shape[0], 4)], axis=0)
    p = jnp.concatenate([every[i + 2 : i + 4] for i in range(0, every.shape[0], 4)], axis=0)
    return q, p


def gram_kernel(a, b, out):
    q, p = split_kinds(a[...], b[...])
    res = exact_dot(q, p, ((1,), (1,)))
    res = jnp.concatenate([res[:8], res[8:], jnp.zeros((8, 96), F32)], axis=1)
    for i in range(out.shape[0]):
        out[i] = res


def gram(a, b, copies):
    return pl.pallas_call(
        gram_kernel,
        out_shape=jax.ShapeDtypeStruct((copies, 8, 128), F32),
        compiler_params=pltpu.CompilerParams(vmem_limit_bytes=4 * MIB),
        name="gram",
    )(a, b)


def nt_dot(a, b):
    return lax.dot_general(a, b, (((1,), (1,)), ((), ())), preferred_element_type=F32)


def store_halves(core, res, mine, sib):
    left, right = res[:, :BLK], res[:, BLK:]

    @pl.when(core == 0)
    def _():
        mine[...] = left
        sib[...] = right.astype(BF)

    @pl.when(core != 0)
    def _():
        mine[...] = right
        sib[...] = left.astype(BF)


def first_grad_kernel(
    seqs, place, total_queries, idx, parts, pa, pb, stats, picked, expo, w, dl, loss, mine, sib, es, ws, esem, wsem
):
    e_copies = [
        pltpu.make_async_copy(expo.at[pl.ds(start, n), :], es.at[pl.ds(start, n), :], esem.at[s])
        for s, (start, n) in enumerate(seqs)
    ]
    row0 = pl.multiple_of(idx[place] * (2 * BLK), 2 * BLK)
    w_copy = pltpu.make_async_copy(w.at[pl.ds(row0, 2 * BLK), :], ws, wsem)
    for c in e_copies:
        c.start()
    w_copy.start()
    scores = parts[0]
    for i in range(1, parts.shape[0]):
        scores = scores + parts[i]
    scores = jnp.concatenate([scores[:, :16], scores[:, 16:32]], axis=0) / DIV
    top = jnp.max(scores, axis=1, keepdims=True)
    lse = top + jnp.log(jnp.sum(jnp.exp(scores - top), axis=1, keepdims=True))
    pick = picked[...]
    losses = lse - jnp.sum(scores * pick, axis=1, keepdims=True)
    loss[...] = jnp.broadcast_to(losses[:8], loss.shape)
    dscores = (jnp.exp(scores - lse) - pick) * (LOSS_SCALE / total_queries)
    q, p = split_kinds(pa[...], pb[...])
    dq = exact_dot(dscores[:8], p, ((1,), (0,)))
    dp = exact_dot(dscores.T[:8], q, ((1,), (0,)))
    dpooled = jnp.concatenate([dq[:2], dp[:2]], axis=0) / DIV
    smooth = stats[0:4, :]
    gate = jnp.where(smooth > 0, 1.0 / (1.0 + jnp.maximum(smooth, 0.0)), 0.0)
    g = dpooled * gate / stats[4:8, :]
    for s, (start, n) in enumerate(seqs):
        e_copies[s].wait()
        dl[pl.ds(start, n), :] = (es[pl.ds(start, n), :].astype(F32) * g[s : s + 1, :]).astype(BF)
    w_copy.wait()
    store_halves(idx[8], nt_dot(dl[...], ws[...]), mine, sib)


def first_grad(place, idx, parts, pa, pb, stats, picked, expo, w, seqs, total_queries):
    rows, cols = expo.shape
    vm = pl.BlockSpec(memory_space=pltpu.VMEM)
    return pl.pallas_call(
        functools.partial(first_grad_kernel, seqs, place, total_queries),
        in_specs=[pl.BlockSpec(memory_space=pltpu.SMEM)] + [vm] * 5 + [HBM_SPEC] * 2,
        out_specs=[vm] * 4,
        scratch_shapes=[
            pltpu.VMEM((rows, cols), BF),
            pltpu.VMEM((2 * BLK, cols), BF),
            pltpu.SemaphoreType.DMA((len(seqs),)),
            pltpu.SemaphoreType.DMA,
        ],
        out_shape=[
            jax.ShapeDtypeStruct((rows, cols), BF),
            jax.ShapeDtypeStruct((8, 128), F32),
            jax.ShapeDtypeStruct((rows, BLK), F32),
            jax.ShapeDtypeStruct((rows, BLK), BF),
        ],
        compiler_params=pltpu.CompilerParams(vmem_limit_bytes=22 * MIB),
        name="first_grad",
        cost_estimate=matmul_cost(rows, 2 * BLK, cols),
    )(idx, parts, pa, pb, stats, picked, pltpu.with_memory_space_constraint(expo, pltpu.HBM), w)


def grad_kernel(first, n, idx, dl, w, mine, sib, ws, wsem):
    i = pl.program_id(0)

    def w_copy(step, slot):
        row = pl.multiple_of(idx[first + step] * (2 * BLK), 2 * BLK)
        return pltpu.make_async_copy(w.at[pl.ds(row, 2 * BLK), :], ws.at[slot], wsem.at[slot])

    slot = lax.rem(i, 2)

    @pl.when(i == 0)
    def _():
        w_copy(0, 0).start()

    @pl.when(i + 1 < n)
    def _():
        w_copy(i + 1, 1 - slot).start()

    w_copy(i, slot).wait()
    store_halves(idx[8], nt_dot(dl[...], ws[slot]), mine, sib)


def grad_part(first, n, idx, dl, w):
    rows, cols = dl.shape
    out = pl.BlockSpec((rows, BLK), lambda i, idx: (i, 0))
    return pl.pallas_call(
        functools.partial(grad_kernel, first, n),
        grid_spec=pltpu.PrefetchScalarGridSpec(
            num_scalar_prefetch=1,
            grid=(n,),
            in_specs=[pl.BlockSpec((rows, cols), lambda i, idx: (0, 0)), HBM_SPEC],
            out_specs=[out, out],
            scratch_shapes=[pltpu.VMEM((2, 2 * BLK, cols), BF), pltpu.SemaphoreType.DMA((2,))],
        ),
        out_shape=[jax.ShapeDtypeStruct((n * rows, BLK), F32), jax.ShapeDtypeStruct((n * rows, BLK), BF)],
        compiler_params=pltpu.CompilerParams(vmem_limit_bytes=18 * MIB),
        name="grad_part",
        cost_estimate=matmul_cost(n * rows, 2 * BLK, cols),
    )(idx, dl, w)


def add_kernel(spec, n_mine, *refs):
    outs = refs[len(refs) - n_mine :]
    for i in range(n_mine):
        outs[i][...] = refs[i][...]
    for i, a, src, dst, n in spec:
        outs[i][pl.ds(dst, n), :] = outs[i][pl.ds(dst, n), :] + refs[n_mine + a][pl.ds(src, n), :].astype(F32)


def add_arrived(mine, arrived, spec):
    return pl.pallas_call(
        functools.partial(add_kernel, spec, len(mine)),
        out_shape=[jax.ShapeDtypeStruct(m.shape, F32) for m in mine],
        compiler_params=pltpu.CompilerParams(vmem_limit_bytes=12 * MIB),
        name="add_arrived",
        cost_estimate=matmul_cost(4096, 2048, 2048),
    )(*mine, *arrived)


def after(x, *others):
    return lax.optimization_barrier((x,) + others)[0]


def on_device(query_hidden, passage_hidden, head_weight, query_mask, passage_mask, positive):
    q_count, q_len, width = query_hidden.shape
    p_count, p_len, _ = passage_hidden.shape
    w = pltpu.with_memory_space_constraint(head_weight, pltpu.HBM)
    split = q_count * q_len
    seqs = tuple((i * q_len, q_len) for i in range(q_count)) + tuple(
        (split + i * p_len, p_len) for i in range(p_count)
    )
    own = jnp.concatenate([query_hidden.reshape(split, width), passage_hidden.reshape(p_count * p_len, width)], axis=0)
    idx = lax.dynamic_index_in_dim(jnp.asarray(place_table()), lax.axis_index("vocab"), 0, keepdims=False)
    at = {p: i for i, p in enumerate(PLACES)}
    h = 384

    x10, xm0, x01 = to_y(own, -1), to_y(own, 1), to_z(own)
    own_s = to_core(own)
    acc = logits_part([own, own_s], ((0, 0, 0, 0, 768), (1, 1, 0, 0, 768)), (0,), idx, w, None)
    x10, xm0, x01, acc = lax.optimization_barrier((x10, xm0, x01, acc))
    f1 = to_y(jnp.concatenate([x10[:h], x01[h:]], axis=0), -1)
    f2 = to_y(jnp.concatenate([x01[h:], xm0[h:]], axis=0), 1)
    f3 = to_z(jnp.concatenate([x10[:h], xm0[:h]], axis=0))
    near = [t for p in (x10, xm0, x01) for t in (p, to_core(p))]
    whole = tuple((i, i, 0, 0, 768) for i in range(6))
    acc = logits_part(near, whole, (1, 2, 3), idx, w, acc, pltpu.HBM)
    f1, f2, f3, acc = lax.optimization_barrier((f1, f2, f3, acc))
    g1 = to_y(f3[:256], -1)
    g2 = to_z(jnp.concatenate([f1[256:384], f2[384:512]], axis=0))
    g3 = to_y(f2[128:384], 1)
    mid = [t for p in (f1, f2, f3) for t in (p, to_core(p))]
    mid_copies = []
    for c in range(2):
        mid_copies += [
            (0 + c, 0 + c, 0, 0, h),
            (2 + c, 0 + c, h, h, h),
            (4 + c, 2 + c, 0, 0, h),
            (0 + c, 2 + c, h, h, h),
            (4 + c, 4 + c, h, 0, h),
            (2 + c, 4 + c, 0, h, h),
        ]
    acc = logits_part(mid, tuple(mid_copies), (4, 5, 6), idx, w, pltpu.with_memory_space_constraint(acc, pltpu.HBM))
    g1, g2, g3, acc = lax.optimization_barrier((g1, g2, g3, acc))
    last = [t for p in (g1, g2, g3) for t in (p, to_core(p))]
    last_copies = tuple((2 * i + c, c, 0, 256 * i, 256) for i in range(3) for c in range(2))
    query_mask, passage_mask, positive = lax.optimization_barrier((query_mask, passage_mask, positive, x10))[:3]
    lens = jnp.concatenate([jnp.sum(query_mask > 0, axis=1), jnp.sum(passage_mask > 0, axis=1)]).astype(jnp.int32)
    expo, stats, pooled = logits_pool(last, last_copies, (7,), idx, lens, w, acc, seqs)

    pa = jnp.concatenate([pooled] + [to_x(pooled, -k) for k in (1, 2, 3)], axis=0)
    pb = to_zhi(pa)
    parts = lax.all_to_all(gram(pa, pb, 16), "vocab", 0, 0)

    group = lax.axis_index("dp")
    slot = jnp.arange(16, dtype=jnp.int32)
    place = slot // 2
    gx = (group // 2 + place % 4) % 4
    gz = (group % 2 + place // 4) % 2
    seq = (gx * 2 + gz) * 2 + slot % 2
    target = positive[seq]
    picked = (target[:, None] == seq[None, :]).astype(F32)

    dl, loss, m21, s21 = first_grad(7, idx, parts, pa, pb, stats, picked, expo, w, seqs, positive.shape[0])
    m20, s20 = grad_part(4, 1, idx, dl, w)
    t21 = (m21 + to_core(s21)).astype(BF)
    def rows(x, i):
        return x[768 * i : 768 * (i + 1)]

    r1, r2, r3 = to_y(t21[:256], 1), to_z(t21[256:512]), to_y(t21[512:], -1)
    mb, sb = grad_part(5, 2, idx, after(dl, t21), w)
    sb = to_core(sb)
    mb, m20 = add_arrived((mb, m20), (r1, r2, r3), ((0, 0, 0, 0, 256), (0, 2, 0, 768 + 512, 256), (1, 1, 0, 256, 256)))
    t20 = (m20 + to_core(s20)).astype(BF)
    t11 = (rows(mb, 0) + rows(sb, 0)).astype(BF)
    tm1 = (rows(mb, 1) + rows(sb, 1)).astype(BF)
    c1 = jnp.concatenate([t20[:h], t11[h:]], axis=0)
    c2 = jnp.concatenate([tm1[h:], t20[h:]], axis=0)
    c3 = jnp.concatenate([t11[:h], tm1[:h]], axis=0)
    c1, c2, c3, dl = lax.optimization_barrier((c1, c2, c3, dl))
    u1, u2, u3 = to_y(c1, 1), to_y(c2, -1), to_z(c3)
    mc, sc = grad_part(1, 3, idx, dl, w)
    sc = to_core(sc)
    (mc,) = add_arrived(
        (mc,),
        (u1, u2, u3),
        (
            (0, 0, 0, 0, h),
            (0, 2, 0, 0, h),
            (0, 2, h, 768, h),
            (0, 1, h, 768 + h, h),
            (0, 0, h, 1536 + h, h),
            (0, 1, 0, 1536 + h, h),
        ),
    )
    t10, tm0, t01 = ((rows(mc, i) + rows(sc, i)).astype(BF) for i in range(3))
    t10, tm0, t01, dl = lax.optimization_barrier((t10, tm0, t01, dl))
    v1, v2, v3 = to_y(t10, 1), to_y(tm0, -1), to_z(t01)
    md, sd = grad_part(0, 1, idx, dl, w)
    k00 = lax.optimization_barrier(md + v1.astype(F32) + v2.astype(F32) + v3.astype(F32))
    sd = to_core(sd)

    def total(a, b):
        return (k00[a:b] + sd[a:b].astype(F32)).astype(BF)

    return (
        total(0, split).reshape(q_count, q_len, width),
        total(split, 768).reshape(p_count, p_len, width),
        loss[:q_count, 0],
    )


def solution(mesh):
    return jax.shard_map(
        on_device,
        mesh=mesh,
        in_specs=(
            P("dp", None, "vocab"),
            P("dp", None, "vocab"),
            P(None, "vocab"),
            P("dp", None),
            P("dp", None),
            P(),
        ),
        out_specs=(P("dp", None, "vocab"), P("dp", None, "vocab"), P("dp")),
        check_vma=False,
    )
```

```python
import functools

import jax
import jax.numpy as jnp
import numpy as np
from jax import lax
from jax.experimental import pallas as pl
from jax.experimental.pallas import tpu as pltpu
from jax.sharding import PartitionSpec as P

SHARP = 0.2
DIV = 16.0
LOSS_SCALE = 65536.0
BF = jnp.bfloat16
F32 = jnp.float32
MIB = 1024 * 1024
BLK = 256
HBM_SPEC = pl.BlockSpec(memory_space=pltpu.HBM)


def y_perm(k):
    return [(z * 8 + y * 2 + c, z * 8 + ((y + k) % 4) * 2 + c) for z in range(2) for y in range(4) for c in range(2)]


Z_SWAP = [(v, v ^ 8) for v in range(16)]
CORE_SWAP = [(v, v ^ 1) for v in range(16)]


def to_y(x, k):
    return lax.ppermute(x, "vocab", y_perm(k % 4))


def to_z(x):
    return lax.ppermute(x, "vocab", Z_SWAP)


def to_core(x):
    return lax.ppermute(x, "vocab", CORE_SWAP)


def to_x(x, k):
    return lax.ppermute(x, "dp", [(g, ((g // 2 + k) % 4) * 2 + g % 2) for g in range(8)])


def to_zhi(x):
    return lax.ppermute(x, "dp", [(g, g ^ 1) for g in range(8)])


PLACES = ((0, 0), (1, 0), (-1, 0), (0, 1), (2, 0), (1, 1), (-1, 1), (2, 1))


def place_table():
    rows = []
    for g in range(8):
        gx, gz = g // 2, g % 2
        seqs = [(((gx + i % 4) % 4) * 2 + (gz + i // 4) % 2) * 2 + k for i in range(8) for k in range(2)]
        for v in range(16):
            z, y, core = v // 8, (v // 2) % 4, v % 2
            rows.append([((z + dz) % 2) * 4 + (y + dy) % 4 for dy, dz in PLACES] + [core] * 8 + seqs)
    return np.array(rows, np.int32)


def matmul_cost(m, k, n):
    return pl.CostEstimate(flops=2 * m * k * n, bytes_accessed=2 * k * n, transcendentals=0)


def load_operands(copies, places, bn, steps, idx, xrefs, w, xs, ws, xsem, wsem):
    j = pl.program_id(0)
    nk = 2 * len(places)

    def x_copy(i):
        a, k, src, dst, n = copies[i]
        return pltpu.make_async_copy(
            xrefs[a].at[pl.ds(src, n), :], xs.at[pl.ds(dst, n), pl.ds(k * BLK, BLK)], xsem.at[i]
        )

    def w_copy(step, slot, k):
        core = idx[8]
        side = core if k % 2 == 0 else 1 - core
        row = pl.multiple_of((idx[places[k // 2]] * 2 + side) * BLK, BLK)
        col = pl.multiple_of(step * bn, bn)
        return pltpu.make_async_copy(
            w.at[pl.ds(row, BLK), pl.ds(col, bn)], ws.at[slot, pl.ds(k * BLK, BLK), :], wsem.at[slot, k]
        )

    slot = lax.rem(j, 2)

    @pl.when(j == 0)
    def _():
        for k in range(nk):
            w_copy(0, 0, k).start()
        for i in range(len(copies)):
            x_copy(i).start()

    @pl.when(j == 0)
    def _():
        for i in range(len(copies)):
            x_copy(i).wait()

    for k in range(nk):
        w_copy(j, slot, k).wait()

    @pl.when(j + 1 < steps)
    def _():
        for k in range(nk):
            w_copy(j + 1, 1 - slot, k).start()

    return slot


def columns_of(bn):
    return pl.ds(pl.multiple_of(pl.program_id(0) * bn, bn), bn)


def logits_kernel(copies, places, nx, bn, steps, has_acc, idx, *refs):
    xrefs = refs[:nx]
    w = refs[nx]
    pos = nx + 1
    acc = None
    if has_acc:
        acc = refs[pos]
        pos += 1
    out, xs, ws, xsem, wsem = refs[pos:]
    slot = load_operands(copies, places, bn, steps, idx, xrefs, w, xs, ws, xsem, wsem)
    res = jnp.dot(xs[...], ws[slot], preferred_element_type=F32)
    cols = columns_of(bn)
    if has_acc:
        res = res + acc[:, cols]
    out[:, cols] = res


def logits_part(arrays, copies, places, idx, w, acc):
    rows = 768
    cols = w.shape[1]
    nk = 2 * len(places)
    bn = 512
    steps = cols // bn
    any_spec = pl.BlockSpec(memory_space=pl.ANY)
    vm = pl.BlockSpec(memory_space=pltpu.VMEM)
    ins = list(arrays) + [w] + ([acc] if acc is not None else [])
    return pl.pallas_call(
        functools.partial(logits_kernel, copies, places, len(arrays), bn, steps, acc is not None),
        grid_spec=pltpu.PrefetchScalarGridSpec(
            num_scalar_prefetch=1,
            grid=(steps,),
            in_specs=[any_spec] * len(arrays) + [HBM_SPEC] + ([vm] if acc is not None else []),
            out_specs=vm,
            scratch_shapes=[
                pltpu.VMEM((rows, nk * BLK), BF),
                pltpu.VMEM((2, nk * BLK, bn), BF),
                pltpu.SemaphoreType.DMA((len(copies),)),
                pltpu.SemaphoreType.DMA((2, nk)),
            ],
        ),
        out_shape=jax.ShapeDtypeStruct((rows, cols), F32),
        input_output_aliases={len(arrays) + 2: 0} if acc is not None else {},
        compiler_params=pltpu.CompilerParams(vmem_limit_bytes=(14 if nk > 2 else 12) * MIB),
        name="logits_part",
    )(idx, *ins)


def pool_kernel(copies, places, nx, bn, steps, seqs, idx, lens, *refs):
    xrefs = refs[:nx]
    w, acc, expo, stats, pooled, xs, ws, xsem, wsem = refs[nx:]
    slot = load_operands(copies, places, bn, steps, idx, xrefs, w, xs, ws, xsem, wsem)
    logits = jnp.dot(xs[...], ws[slot], preferred_element_type=F32) + acc[:, columns_of(bn)]
    smooth, sums = [], []
    for s, (start, n) in enumerate(seqs):
        part = logits[start : start + n] * (1.0 / SHARP)
        live = lax.broadcasted_iota(jnp.int32, (n, 1), 0) < lens[s]
        part = jnp.where(live, part, -1e30)
        top = jnp.max(part, axis=0, keepdims=True)
        e = jnp.exp(part - top)
        total = jnp.sum(e, axis=0, keepdims=True)
        expo[pl.ds(start, n), :] = e.astype(BF)
        smooth.append(SHARP * (top + jnp.log(total)))
        sums.append(total)
    both = jnp.concatenate(smooth + sums, axis=0)
    stats[...] = both
    pooled[...] = jnp.log1p(jnp.maximum(both[:4], 0.0))


def logits_pool(arrays, copies, places, idx, lens, w, acc, seqs):
    rows = 768
    cols = w.shape[1]
    nk = 2 * len(places)
    bn = 512
    steps = cols // bn
    any_spec = pl.BlockSpec(memory_space=pl.ANY)
    blk = pl.BlockSpec((rows, bn), lambda j, *_: (0, j))
    return pl.pallas_call(
        functools.partial(pool_kernel, copies, places, len(arrays), bn, steps, seqs),
        grid_spec=pltpu.PrefetchScalarGridSpec(
            num_scalar_prefetch=2,
            grid=(steps,),
            in_specs=[any_spec] * len(arrays) + [HBM_SPEC, pl.BlockSpec(memory_space=pltpu.VMEM)],
            out_specs=[
                blk,
                pl.BlockSpec((8, bn), lambda j, *_: (0, j)),
                pl.BlockSpec((4, bn), lambda j, *_: (0, j)),
            ],
            scratch_shapes=[
                pltpu.VMEM((rows, nk * BLK), BF),
                pltpu.VMEM((2, nk * BLK, bn), BF),
                pltpu.SemaphoreType.DMA((len(copies),)),
                pltpu.SemaphoreType.DMA((2, nk)),
            ],
        ),
        out_shape=[
            pltpu.HBM((rows, cols), BF),
            jax.ShapeDtypeStruct((8, cols), F32),
            jax.ShapeDtypeStruct((4, cols), F32),
        ],
        compiler_params=pltpu.CompilerParams(vmem_limit_bytes=16 * MIB),
        name="logits_pool",
    )(idx, lens, *arrays, w, acc)


def exact_dot(a, b, dims):
    return lax.dot_general(a, b, (dims, ((), ())), precision=lax.Precision.HIGHEST, preferred_element_type=F32)


def split_kinds(a, b):
    every = jnp.concatenate([a, b], axis=0)
    q = jnp.concatenate([every[i : i + 2] for i in range(0, every.shape[0], 4)], axis=0)
    p = jnp.concatenate([every[i + 2 : i + 4] for i in range(0, every.shape[0], 4)], axis=0)
    return q, p


def gram_kernel(a, b, out):
    q, p = split_kinds(a[...], b[...])
    res = exact_dot(q, p, ((1,), (1,)))
    res = jnp.concatenate([res[:8], res[8:], jnp.zeros((8, 96), F32)], axis=1)
    for i in range(out.shape[0]):
        out[i] = res


def gram(a, b, copies):
    return pl.pallas_call(
        gram_kernel,
        out_shape=jax.ShapeDtypeStruct((copies, 8, 128), F32),
        compiler_params=pltpu.CompilerParams(vmem_limit_bytes=4 * MIB),
        name="gram",
    )(a, b)


def nt_dot(a, b):
    return lax.dot_general(a, b, (((1,), (1,)), ((), ())), preferred_element_type=F32)


def store_halves(core, res, mine, sib):
    left, right = res[:, :BLK], res[:, BLK:]

    @pl.when(core == 0)
    def _():
        mine[...] = left
        sib[...] = right.astype(BF)

    @pl.when(core != 0)
    def _():
        mine[...] = right
        sib[...] = left.astype(BF)


def first_grad_kernel(
    seqs, place, total_queries, idx, parts, pa, pb, stats, picked, expo, w, dl, loss, mine, sib, es, ws, esem, wsem
):
    e_copies = [
        pltpu.make_async_copy(expo.at[pl.ds(start, n), :], es.at[pl.ds(start, n), :], esem.at[s])
        for s, (start, n) in enumerate(seqs)
    ]
    row0 = pl.multiple_of(idx[place] * (2 * BLK), 2 * BLK)
    w_copy = pltpu.make_async_copy(w.at[pl.ds(row0, 2 * BLK), :], ws, wsem)
    for c in e_copies:
        c.start()
    w_copy.start()
    scores = parts[0]
    for i in range(1, parts.shape[0]):
        scores = scores + parts[i]
    scores = jnp.concatenate([scores[:, :16], scores[:, 16:32]], axis=0) / DIV
    top = jnp.max(scores, axis=1, keepdims=True)
    lse = top + jnp.log(jnp.sum(jnp.exp(scores - top), axis=1, keepdims=True))
    pick = picked[...]
    losses = lse - jnp.sum(scores * pick, axis=1, keepdims=True)
    loss[...] = jnp.broadcast_to(losses[:8], loss.shape)
    dscores = (jnp.exp(scores - lse) - pick) * (LOSS_SCALE / total_queries)
    q, p = split_kinds(pa[...], pb[...])
    dq = exact_dot(dscores[:8], p, ((1,), (0,)))
    dp = exact_dot(dscores.T[:8], q, ((1,), (0,)))
    dpooled = jnp.concatenate([dq[:2], dp[:2]], axis=0) / DIV
    smooth = stats[0:4, :]
    gate = jnp.where(smooth > 0, 1.0 / (1.0 + jnp.maximum(smooth, 0.0)), 0.0)
    g = dpooled * gate / stats[4:8, :]
    for s, (start, n) in enumerate(seqs):
        e_copies[s].wait()
        dl[pl.ds(start, n), :] = (es[pl.ds(start, n), :].astype(F32) * g[s : s + 1, :]).astype(BF)
    w_copy.wait()
    store_halves(idx[8], nt_dot(dl[...], ws[...]), mine, sib)


def first_grad(place, idx, parts, pa, pb, stats, picked, expo, w, seqs, total_queries):
    rows, cols = expo.shape
    vm = pl.BlockSpec(memory_space=pltpu.VMEM)
    return pl.pallas_call(
        functools.partial(first_grad_kernel, seqs, place, total_queries),
        in_specs=[pl.BlockSpec(memory_space=pltpu.SMEM)] + [vm] * 5 + [HBM_SPEC] * 2,
        out_specs=[vm] * 4,
        scratch_shapes=[
            pltpu.VMEM((rows, cols), BF),
            pltpu.VMEM((2 * BLK, cols), BF),
            pltpu.SemaphoreType.DMA((len(seqs),)),
            pltpu.SemaphoreType.DMA,
        ],
        out_shape=[
            jax.ShapeDtypeStruct((rows, cols), BF),
            jax.ShapeDtypeStruct((8, 128), F32),
            jax.ShapeDtypeStruct((rows, BLK), F32),
            jax.ShapeDtypeStruct((rows, BLK), BF),
        ],
        compiler_params=pltpu.CompilerParams(vmem_limit_bytes=18 * MIB),
        name="first_grad",
    )(idx, parts, pa, pb, stats, picked, pltpu.with_memory_space_constraint(expo, pltpu.HBM), w)


def grad_kernel(first, n, idx, dl, w, mine, sib, ws, wsem):
    i = pl.program_id(0)

    def w_copy(step, slot):
        row = pl.multiple_of(idx[first + step] * (2 * BLK), 2 * BLK)
        return pltpu.make_async_copy(w.at[pl.ds(row, 2 * BLK), :], ws.at[slot], wsem.at[slot])

    slot = lax.rem(i, 2)

    @pl.when(i == 0)
    def _():
        w_copy(0, 0).start()

    @pl.when(i + 1 < n)
    def _():
        w_copy(i + 1, 1 - slot).start()

    w_copy(i, slot).wait()
    store_halves(idx[8], nt_dot(dl[...], ws[slot]), mine, sib)


def grad_part(first, n, idx, dl, w):
    rows, cols = dl.shape
    out = pl.BlockSpec((rows, BLK), lambda i, idx: (i, 0))
    return pl.pallas_call(
        functools.partial(grad_kernel, first, n),
        grid_spec=pltpu.PrefetchScalarGridSpec(
            num_scalar_prefetch=1,
            grid=(n,),
            in_specs=[pl.BlockSpec(memory_space=pltpu.VMEM), HBM_SPEC],
            out_specs=[out, out],
            scratch_shapes=[pltpu.VMEM((2, 2 * BLK, cols), BF), pltpu.SemaphoreType.DMA((2,))],
        ),
        out_shape=[jax.ShapeDtypeStruct((n * rows, BLK), F32), jax.ShapeDtypeStruct((n * rows, BLK), BF)],
        compiler_params=pltpu.CompilerParams(vmem_limit_bytes=12 * MIB),
        name="grad_part",
    )(idx, dl, w)


def add_kernel(spec, n_mine, *refs):
    outs = refs[len(refs) - n_mine :]
    for i in range(n_mine):
        outs[i][...] = refs[i][...]
    for i, a, src, dst, n in spec:
        outs[i][pl.ds(dst, n), :] = outs[i][pl.ds(dst, n), :] + refs[n_mine + a][pl.ds(src, n), :].astype(F32)


def add_arrived(mine, arrived, spec):
    return pl.pallas_call(
        functools.partial(add_kernel, spec, len(mine)),
        out_shape=[jax.ShapeDtypeStruct(m.shape, F32) for m in mine],
        compiler_params=pltpu.CompilerParams(vmem_limit_bytes=12 * MIB),
        name="add_arrived",
        cost_estimate=matmul_cost(4096, 2048, 2048),
    )(*mine, *arrived)


def add_last_kernel(split, *refs):
    parts, (out_q, out_p) = refs[:-2], refs[-2:]
    res = parts[0][...]
    for p in parts[1:]:
        res = res + p[...].astype(F32)
    res = res.astype(BF)
    out_q[...] = res[:split]
    out_p[...] = res[split:]


def add_last(mine, others, split):
    rows, cols = mine.shape
    return pl.pallas_call(
        functools.partial(add_last_kernel, split),
        out_shape=[jax.ShapeDtypeStruct((split, cols), BF), jax.ShapeDtypeStruct((rows - split, cols), BF)],
        compiler_params=pltpu.CompilerParams(vmem_limit_bytes=12 * MIB),
        name="add_last",
    )(mine, *others)


def after(x, *others):
    return lax.optimization_barrier((x,) + others)[0]


def on_device(query_hidden, passage_hidden, head_weight, query_mask, passage_mask, positive):
    q_count, q_len, width = query_hidden.shape
    p_count, p_len, _ = passage_hidden.shape
    w = pltpu.with_memory_space_constraint(head_weight, pltpu.HBM)
    split = q_count * q_len
    seqs = tuple((i * q_len, q_len) for i in range(q_count)) + tuple(
        (split + i * p_len, p_len) for i in range(p_count)
    )
    own = jnp.concatenate([query_hidden.reshape(split, width), passage_hidden.reshape(p_count * p_len, width)], axis=0)
    me = lax.axis_index(("dp", "vocab"))
    idx = lax.dynamic_index_in_dim(jnp.asarray(place_table()), me, 0, keepdims=False)
    at = {p: i for i, p in enumerate(PLACES)}
    h = 384

    x10, xm0, x01 = to_y(own, -1), to_y(own, 1), to_z(own)
    own_s = to_core(own)
    acc = logits_part([own, own_s], ((0, 0, 0, 0, 768), (1, 1, 0, 0, 768)), (0,), idx, w, None)
    x10, xm0, x01, acc = lax.optimization_barrier((x10, xm0, x01, acc))
    f1 = to_y(jnp.concatenate([x10[:h], x01[h:]], axis=0), -1)
    f2 = to_y(jnp.concatenate([x01[h:], xm0[h:]], axis=0), 1)
    f3 = to_z(jnp.concatenate([x10[:h], xm0[:h]], axis=0))
    near = [t for p in (x10, xm0, x01) for t in (p, to_core(p))]
    whole = tuple((i, i, 0, 0, 768) for i in range(6))
    acc = logits_part(near, whole, (1, 2, 3), idx, w, acc)
    f1, f2, f3, acc = lax.optimization_barrier((f1, f2, f3, acc))
    g1 = to_y(f3[:h], -1)
    g2 = to_z(f2[h:])
    mid = [t for p in (f1, f2, f3) for t in (p, to_core(p))]
    mid_copies = []
    for c in range(2):
        mid_copies += [
            (0 + c, 0 + c, 0, 0, h),
            (2 + c, 0 + c, h, h, h),
            (4 + c, 2 + c, 0, 0, h),
            (0 + c, 2 + c, h, h, h),
            (4 + c, 4 + c, h, 0, h),
            (2 + c, 4 + c, 0, h, h),
        ]
    acc = logits_part(mid, tuple(mid_copies), (4, 5, 6), idx, w, acc)
    g1, g2, acc = lax.optimization_barrier((g1, g2, acc))
    last = [t for p in (g1, g2) for t in (p, to_core(p))]
    last_copies = tuple((2 * i + c, c, 0, h * i, h) for i in range(2) for c in range(2))
    query_mask, passage_mask, positive = lax.optimization_barrier((query_mask, passage_mask, positive, x10))[:3]
    lens = jnp.concatenate([jnp.sum(query_mask > 0, axis=1), jnp.sum(passage_mask > 0, axis=1)]).astype(jnp.int32)
    expo, stats, pooled = logits_pool(last, last_copies, (7,), idx, lens, w, acc, seqs)

    pa = jnp.concatenate([pooled] + [to_x(pooled, -k) for k in (1, 2, 3)], axis=0)
    pb = to_zhi(pa)
    parts = lax.all_to_all(gram(pa, pb, 16), "vocab", 0, 0)

    seq = idx[16:]
    target = positive[seq]
    picked = (target[:, None] == seq[None, :]).astype(F32)

    dl, loss, m21, s21 = first_grad(7, idx, parts, pa, pb, stats, picked, expo, w, seqs, positive.shape[0])
    t21 = (m21 + to_core(s21)).astype(BF)
    def rows(x, i):
        return x[768 * i : 768 * (i + 1)]

    r1, r2 = to_y(t21[:h], 1), to_z(t21[h:])
    mb, sb = grad_part(4, 3, idx, after(dl, t21), w)
    sb = to_core(sb)
    (mb,) = add_arrived((mb,), (r1, r2), ((0, 0, 0, 768, h), (0, 1, 0, h, h)))
    t20, t11, tm1 = ((rows(mb, i) + rows(sb, i)).astype(BF) for i in range(3))
    c1 = jnp.concatenate([t20[:h], t11[h:]], axis=0)
    c2 = jnp.concatenate([tm1[h:], t20[h:]], axis=0)
    c3 = jnp.concatenate([t11[:h], tm1[:h]], axis=0)
    c1, c2, c3, dl = lax.optimization_barrier((c1, c2, c3, dl))
    u1, u2, u3 = to_y(c1, 1), to_y(c2, -1), to_z(c3)
    mc, sc = grad_part(1, 3, idx, dl, w)
    sc = to_core(sc)
    (mc,) = add_arrived(
        (mc,),
        (u1, u2, u3),
        (
            (0, 0, 0, 0, h),
            (0, 2, 0, 0, h),
            (0, 2, h, 768, h),
            (0, 1, h, 768 + h, h),
            (0, 0, h, 1536 + h, h),
            (0, 1, 0, 1536 + h, h),
        ),
    )
    t10, tm0, t01 = ((rows(mc, i) + rows(sc, i)).astype(BF) for i in range(3))
    t10, tm0, t01, dl = lax.optimization_barrier((t10, tm0, t01, dl))
    v1, v2, v3 = to_y(t10, 1), to_y(tm0, -1), to_z(t01)
    md, sd = grad_part(0, 1, idx, dl, w)
    (md,) = add_arrived((md,), (v1, v2, v3), tuple((0, i, 0, 0, 768) for i in range(3)))
    out_q, out_p = add_last(md, (to_core(sd),), split)
    return (
        out_q.reshape(q_count, q_len, width),
        out_p.reshape(p_count, p_len, width),
        loss[:q_count, 0],
    )


def solution(mesh):
    return jax.shard_map(
        on_device,
        mesh=mesh,
        in_specs=(
            P("dp", None, "vocab"),
            P("dp", None, "vocab"),
            P(None, "vocab"),
            P("dp", None),
            P("dp", None),
            P(),
        ),
        out_specs=(P("dp", None, "vocab"), P("dp", None, "vocab"), P("dp")),
        check_vma=False,
    )
```

```python
import functools

import jax
import jax.numpy as jnp
import numpy as np
from jax import lax
from jax.experimental import pallas as pl
from jax.experimental.pallas import tpu as pltpu
from jax.sharding import PartitionSpec as P

SHARP = 0.2
DIV = 16.0
LOSS_SCALE = 65536.0
BF = jnp.bfloat16
F32 = jnp.float32
MIB = 1024 * 1024
BLK = 256
HBM_SPEC = pl.BlockSpec(memory_space=pltpu.HBM)


def y_perm(k):
    return [(z * 8 + y * 2 + c, z * 8 + ((y + k) % 4) * 2 + c) for z in range(2) for y in range(4) for c in range(2)]


Z_SWAP = [(v, v ^ 8) for v in range(16)]
CORE_SWAP = [(v, v ^ 1) for v in range(16)]


def to_y(x, k):
    return lax.ppermute(x, "vocab", y_perm(k % 4))


def to_z(x):
    return lax.ppermute(x, "vocab", Z_SWAP)


def to_core(x):
    return lax.ppermute(x, "vocab", CORE_SWAP)


def to_x(x, k):
    return lax.ppermute(x, "dp", [(g, ((g // 2 + k) % 4) * 2 + g % 2) for g in range(8)])


def to_zhi(x):
    return lax.ppermute(x, "dp", [(g, g ^ 1) for g in range(8)])


PLACES = ((0, 0), (1, 0), (-1, 0), (0, 1), (2, 0), (1, 1), (-1, 1), (2, 1))


def place_table():
    rows = []
    for g in range(8):
        gx, gz = g // 2, g % 2
        seqs = [(((gx + i % 4) % 4) * 2 + (gz + i // 4) % 2) * 2 + k for i in range(8) for k in range(2)]
        for v in range(16):
            z, y, core = v // 8, (v // 2) % 4, v % 2
            rows.append([((z + dz) % 2) * 4 + (y + dy) % 4 for dy, dz in PLACES] + [core] * 8 + seqs)
    return np.array(rows, np.int32)


def matmul_cost(m, k, n):
    return pl.CostEstimate(flops=2 * m * k * n, bytes_accessed=2 * k * n, transcendentals=0)


def load_operands(copies, places, bn, steps, idx, xrefs, w, xs, ws, xsem, wsem):
    j = pl.program_id(0)
    nk = 2 * len(places)

    def x_copy(i):
        a, k, src, dst, n = copies[i]
        return pltpu.make_async_copy(
            xrefs[a].at[pl.ds(src, n), :], xs.at[pl.ds(dst, n), pl.ds(k * BLK, BLK)], xsem.at[i]
        )

    def w_copy(step, slot, k):
        core = idx[8]
        side = core if k % 2 == 0 else 1 - core
        row = pl.multiple_of((idx[places[k // 2]] * 2 + side) * BLK, BLK)
        col = pl.multiple_of(step * bn, bn)
        return pltpu.make_async_copy(
            w.at[pl.ds(row, BLK), pl.ds(col, bn)], ws.at[slot, pl.ds(k * BLK, BLK), :], wsem.at[slot, k]
        )

    slot = lax.rem(j, 2)

    @pl.when(j == 0)
    def _():
        for k in range(nk):
            w_copy(0, 0, k).start()
        for i in range(len(copies)):
            x_copy(i).start()

    @pl.when(j == 0)
    def _():
        for i in range(len(copies)):
            x_copy(i).wait()

    for k in range(nk):
        w_copy(j, slot, k).wait()

    @pl.when(j + 1 < steps)
    def _():
        for k in range(nk):
            w_copy(j + 1, 1 - slot, k).start()

    return slot


def columns_of(bn):
    return pl.ds(pl.multiple_of(pl.program_id(0) * bn, bn), bn)


def logits_kernel(copies, places, nx, bn, steps, has_acc, following, idx, *refs):
    xrefs = refs[:nx]
    w = refs[nx]
    pos = nx + 1
    acc = None
    if has_acc:
        acc = refs[pos]
        pos += 1
    out = refs[pos]
    if following is not None:
        ahead, asem = refs[pos + 1], refs[-1]
        refs = refs[:-1]
        ahead_copies = [
            pltpu.make_async_copy(
                w.at[pl.ds(pl.multiple_of((idx[following] * 2 + side) * BLK, BLK), BLK), :],
                ahead.at[pl.ds(k * BLK, BLK), :],
                asem.at[k],
            )
            for k, side in enumerate((idx[8], 1 - idx[8]))
        ]
    xs, ws, xsem, wsem = refs[-4:]
    slot = load_operands(copies, places, bn, steps, idx, xrefs, w, xs, ws, xsem, wsem)
    if following is not None:

        @pl.when(pl.program_id(0) == 0)
        def _():
            for c in ahead_copies:
                c.start()

        @pl.when(pl.program_id(0) == steps - 1)
        def _():
            for c in ahead_copies:
                c.wait()

    res = jnp.dot(xs[...], ws[slot], preferred_element_type=F32)
    cols = columns_of(bn)
    if has_acc:
        res = res + acc[:, cols]
    out[:, cols] = res


def logits_part(arrays, copies, places, idx, w, acc, following=None):
    rows = 768
    cols = w.shape[1]
    nk = 2 * len(places)
    bn = 512
    steps = cols // bn
    any_spec = pl.BlockSpec(memory_space=pl.ANY)
    vm = pl.BlockSpec(memory_space=pltpu.VMEM)
    ins = list(arrays) + [w] + ([acc] if acc is not None else [])
    return pl.pallas_call(
        functools.partial(logits_kernel, copies, places, len(arrays), bn, steps, acc is not None, following),
        grid_spec=pltpu.PrefetchScalarGridSpec(
            num_scalar_prefetch=1,
            grid=(steps,),
            in_specs=[any_spec] * len(arrays) + [HBM_SPEC] + ([vm] if acc is not None else []),
            out_specs=[vm] * (1 if following is None else 2),
            scratch_shapes=[
                pltpu.VMEM((rows, nk * BLK), BF),
                pltpu.VMEM((2, nk * BLK, bn), BF),
                pltpu.SemaphoreType.DMA((len(copies),)),
                pltpu.SemaphoreType.DMA((2, nk)),
            ]
            + ([] if following is None else [pltpu.SemaphoreType.DMA((2,))]),
        ),
        out_shape=[jax.ShapeDtypeStruct((rows, cols), F32)]
        + ([] if following is None else [jax.ShapeDtypeStruct((2 * BLK, cols), BF)]),
        input_output_aliases={len(arrays) + 2: 0} if acc is not None else {},
        compiler_params=pltpu.CompilerParams(vmem_limit_bytes=(14 if nk > 2 else 12) * MIB),
        name="logits_part",
    )(idx, *ins)


def pool_kernel(copies, nx, bn, seqs, lens, *refs):
    xrefs = refs[:nx]
    ws, acc, expo, stats, pooled, xs, es, xsem, esem = refs[nx:]
    steps = ws.shape[1] // bn
    loads = []
    for i, (a, k, src, dst, n) in enumerate(copies):
        loads.append(
            pltpu.make_async_copy(
                xrefs[a].at[pl.ds(src, n), :], xs.at[pl.ds(dst, n), pl.ds(k * BLK, BLK)], xsem.at[i]
            )
        )
    for c in loads:
        c.start()
    for c in loads:
        c.wait()
    outs = []
    for j in range(steps):
        cols = pl.ds(j * bn, bn)
        logits = jnp.dot(xs[...], ws[:, cols], preferred_element_type=F32) + acc[:, cols]
        smooth, sums = [], []
        for s, (start, n) in enumerate(seqs):
            live = lax.broadcasted_iota(jnp.int32, (n, 1), 0) < lens[s]
            part = jnp.where(live, logits[start : start + n], -1e30)
            top = jnp.max(part, axis=0, keepdims=True)
            e = jnp.exp((part - top) * (1.0 / SHARP))
            total = jnp.sum(e, axis=0, keepdims=True)
            es[pl.ds(start, n), cols] = e.astype(BF)
            smooth.append(top + SHARP * jnp.log(total))
            sums.append(total)
        both = jnp.concatenate(smooth + sums, axis=0)
        stats[:, cols] = both
        pooled[:, cols] = jnp.log1p(jnp.maximum(both[:4], 0.0))
        out = pltpu.make_async_copy(es.at[:, cols], expo.at[:, cols], esem.at[j])
        out.start()
        outs.append(out)
    for out in outs:
        out.wait()


def logits_pool(arrays, copies, lens, w, acc, seqs):
    rows = 768
    cols = w.shape[1]
    bn = 512
    any_spec = pl.BlockSpec(memory_space=pl.ANY)
    vm = pl.BlockSpec(memory_space=pltpu.VMEM)
    sm = pl.BlockSpec(memory_space=pltpu.SMEM)
    return pl.pallas_call(
        functools.partial(pool_kernel, copies, len(arrays), bn, seqs),
        in_specs=[sm] + [any_spec] * len(arrays) + [vm, vm],
        out_specs=[HBM_SPEC, vm, vm],
        scratch_shapes=[
            pltpu.VMEM((rows, 2 * BLK), BF),
            pltpu.VMEM((rows, cols), BF),
            pltpu.SemaphoreType.DMA((len(copies),)),
            pltpu.SemaphoreType.DMA((cols // bn,)),
        ],
        out_shape=[
            pltpu.HBM((rows, cols), BF),
            jax.ShapeDtypeStruct((8, cols), F32),
            jax.ShapeDtypeStruct((4, cols), F32),
        ],
        compiler_params=pltpu.CompilerParams(vmem_limit_bytes=16 * MIB),
        name="logits_pool",
    )(lens, *arrays, w, acc)


def exact_dot(a, b, dims):
    return lax.dot_general(a, b, (dims, ((), ())), precision=lax.Precision.HIGHEST, preferred_element_type=F32)


def split_kinds(a, b):
    every = jnp.concatenate([a, b], axis=0)
    q = jnp.concatenate([every[i : i + 2] for i in range(0, every.shape[0], 4)], axis=0)
    p = jnp.concatenate([every[i + 2 : i + 4] for i in range(0, every.shape[0], 4)], axis=0)
    return q, p


def gram_kernel(a, b, out):
    q, p = split_kinds(a[...], b[...])
    res = exact_dot(q, p, ((1,), (1,)))
    res = jnp.concatenate([res[:8], res[8:], jnp.zeros((8, 96), F32)], axis=1)
    for i in range(out.shape[0]):
        out[i] = res


def gram(a, b, copies):
    return pl.pallas_call(
        gram_kernel,
        out_shape=jax.ShapeDtypeStruct((copies, 8, 128), F32),
        compiler_params=pltpu.CompilerParams(vmem_limit_bytes=4 * MIB),
        name="gram",
    )(a, b)


def nt_dot(a, b):
    return lax.dot_general(a, b, (((1,), (1,)), ((), ())), preferred_element_type=F32)


def store_halves(core, res, mine, sib):
    left, right = res[:, :BLK], res[:, BLK:]

    @pl.when(core == 0)
    def _():
        mine[...] = left
        sib[...] = right.astype(BF)

    @pl.when(core != 0)
    def _():
        mine[...] = right
        sib[...] = left.astype(BF)


def first_grad_kernel(
    seqs, place, following, total_queries, idx, parts, pa, pb, stats, picked, expo, w, dl, loss, mine, sib, ahead, es, ws, esem, wsem
):
    e_copies = [
        pltpu.make_async_copy(expo.at[pl.ds(start, n), :], es.at[pl.ds(start, n), :], esem.at[s])
        for s, (start, n) in enumerate(seqs)
    ]
    row0 = pl.multiple_of(idx[place] * (2 * BLK), 2 * BLK)
    w_copy = pltpu.make_async_copy(w.at[pl.ds(row0, 2 * BLK), :], ws, wsem.at[0])
    row1 = pl.multiple_of(idx[following] * (2 * BLK), 2 * BLK)
    ahead_copy = pltpu.make_async_copy(w.at[pl.ds(row1, 2 * BLK), :], ahead, wsem.at[1])
    for c in e_copies:
        c.start()
    w_copy.start()
    ahead_copy.start()
    scores = parts[0]
    for i in range(1, parts.shape[0]):
        scores = scores + parts[i]
    scores = jnp.concatenate([scores[:, :16], scores[:, 16:32]], axis=0) / DIV
    top = jnp.max(scores, axis=1, keepdims=True)
    lse = top + jnp.log(jnp.sum(jnp.exp(scores - top), axis=1, keepdims=True))
    pick = picked[...]
    losses = lse - jnp.sum(scores * pick, axis=1, keepdims=True)
    loss[...] = jnp.broadcast_to(losses[:8], loss.shape)
    dscores = (jnp.exp(scores - lse) - pick) * (LOSS_SCALE / total_queries)
    q, p = split_kinds(pa[...], pb[...])
    dq = exact_dot(dscores[:8], p, ((1,), (0,)))
    dp = exact_dot(dscores.T[:8], q, ((1,), (0,)))
    dpooled = jnp.concatenate([dq[:2], dp[:2]], axis=0) / DIV
    smooth = stats[0:4, :]
    gate = jnp.where(smooth > 0, 1.0 / (1.0 + jnp.maximum(smooth, 0.0)), 0.0)
    g = dpooled * gate / stats[4:8, :]
    for s, (start, n) in enumerate(seqs):
        e_copies[s].wait()
        dl[pl.ds(start, n), :] = (es[pl.ds(start, n), :].astype(F32) * g[s : s + 1, :]).astype(BF)
    w_copy.wait()
    store_halves(idx[8], nt_dot(dl[...], ws[...]), mine, sib)
    ahead_copy.wait()


def first_grad(place, following, idx, parts, pa, pb, stats, picked, expo, w, seqs, total_queries):
    rows, cols = expo.shape
    vm = pl.BlockSpec(memory_space=pltpu.VMEM)
    return pl.pallas_call(
        functools.partial(first_grad_kernel, seqs, place, following, total_queries),
        in_specs=[pl.BlockSpec(memory_space=pltpu.SMEM)] + [vm] * 5 + [HBM_SPEC] * 2,
        out_specs=[vm] * 5,
        scratch_shapes=[
            pltpu.VMEM((rows, cols), BF),
            pltpu.VMEM((2 * BLK, cols), BF),
            pltpu.SemaphoreType.DMA((len(seqs),)),
            pltpu.SemaphoreType.DMA((2,)),
        ],
        out_shape=[
            jax.ShapeDtypeStruct((rows, cols), BF),
            jax.ShapeDtypeStruct((8, 128), F32),
            jax.ShapeDtypeStruct((rows, BLK), F32),
            jax.ShapeDtypeStruct((rows, BLK), BF),
            jax.ShapeDtypeStruct((2 * BLK, cols), BF),
        ],
        compiler_params=pltpu.CompilerParams(vmem_limit_bytes=18 * MIB),
        name="first_grad",
    )(idx, parts, pa, pb, stats, picked, pltpu.with_memory_space_constraint(expo, pltpu.HBM), w)


def grad_kernel(first, n, has_ahead, idx, dl, w, *refs):
    ahead = refs[0] if has_ahead else None
    mine, sib, ws, wsem = refs[has_ahead:]

    def w_copy(step):
        row = pl.multiple_of(idx[first + step] * (2 * BLK), 2 * BLK)
        return pltpu.make_async_copy(w.at[pl.ds(row, 2 * BLK), :], ws.at[step - has_ahead], wsem.at[step - has_ahead])

    for i in range(has_ahead, n):
        w_copy(i).start()
    rows = dl.shape[0]
    for i in range(n):
        here = pl.ds(i * rows, rows)
        if i < has_ahead:
            block = ahead[...]
        else:
            w_copy(i).wait()
            block = ws[i - has_ahead]
        store_halves(idx[8], nt_dot(dl[...], block), mine.at[here], sib.at[here])


def grad_part(first, n, idx, dl, w, ahead=None):
    rows, cols = dl.shape
    vm = pl.BlockSpec(memory_space=pltpu.VMEM)
    has = 0 if ahead is None else 1
    return pl.pallas_call(
        functools.partial(grad_kernel, first, n, has),
        in_specs=[pl.BlockSpec(memory_space=pltpu.SMEM), vm, HBM_SPEC] + [vm] * has,
        out_specs=[vm, vm],
        scratch_shapes=[pltpu.VMEM((n - has, 2 * BLK, cols), BF), pltpu.SemaphoreType.DMA((n - has,))],
        out_shape=[jax.ShapeDtypeStruct((n * rows, BLK), F32), jax.ShapeDtypeStruct((n * rows, BLK), BF)],
        compiler_params=pltpu.CompilerParams(vmem_limit_bytes=16 * MIB),
        name="grad_part",
    )(idx, dl, w, *([ahead] if has else []))


def add_kernel(spec, n_mine, *refs):
    outs = refs[len(refs) - n_mine :]
    for i in range(n_mine):
        outs[i][...] = refs[i][...]
    for i, a, src, dst, n in spec:
        outs[i][pl.ds(dst, n), :] = outs[i][pl.ds(dst, n), :] + refs[n_mine + a][pl.ds(src, n), :].astype(F32)


def add_arrived(mine, arrived, spec):
    return pl.pallas_call(
        functools.partial(add_kernel, spec, len(mine)),
        out_shape=[jax.ShapeDtypeStruct(m.shape, F32) for m in mine],
        compiler_params=pltpu.CompilerParams(vmem_limit_bytes=12 * MIB),
        name="add_arrived",
        cost_estimate=matmul_cost(4096, 2048, 2048),
    )(*mine, *arrived)


def add_last_kernel(split, *refs):
    parts, (out_q, out_p) = refs[:-2], refs[-2:]
    res = parts[0][...]
    for p in parts[1:]:
        res = res + p[...].astype(F32)
    res = res.astype(BF)
    out_q[...] = res[:split]
    out_p[...] = res[split:]


def add_last(mine, others, split):
    rows, cols = mine.shape
    return pl.pallas_call(
        functools.partial(add_last_kernel, split),
        out_shape=[jax.ShapeDtypeStruct((split, cols), BF), jax.ShapeDtypeStruct((rows - split, cols), BF)],
        compiler_params=pltpu.CompilerParams(vmem_limit_bytes=12 * MIB),
        name="add_last",
    )(mine, *others)


def after(x, *others):
    return lax.optimization_barrier((x,) + others)[0]


def on_device(query_hidden, passage_hidden, head_weight, query_mask, passage_mask, positive):
    q_count, q_len, width = query_hidden.shape
    p_count, p_len, _ = passage_hidden.shape
    w = pltpu.with_memory_space_constraint(head_weight, pltpu.HBM)
    split = q_count * q_len
    seqs = tuple((i * q_len, q_len) for i in range(q_count)) + tuple(
        (split + i * p_len, p_len) for i in range(p_count)
    )
    own = jnp.concatenate([query_hidden.reshape(split, width), passage_hidden.reshape(p_count * p_len, width)], axis=0)
    me = lax.axis_index(("dp", "vocab"))
    idx = lax.dynamic_index_in_dim(jnp.asarray(place_table()), me, 0, keepdims=False)
    at = {p: i for i, p in enumerate(PLACES)}
    h = 384

    x10, xm0, x01 = to_y(own, -1), to_y(own, 1), to_z(own)
    own_s = to_core(own)
    acc = logits_part([own, own_s], ((0, 0, 0, 0, 768), (1, 1, 0, 0, 768)), (0,), idx, w, None)[0]
    x10, xm0, x01, acc = lax.optimization_barrier((x10, xm0, x01, acc))
    f1 = to_y(jnp.concatenate([x10[:h], x01[h:]], axis=0), -1)
    f2 = to_y(jnp.concatenate([x01[h:], xm0[h:]], axis=0), 1)
    f3 = to_z(jnp.concatenate([x10[:h], xm0[:h]], axis=0))
    near = [t for p in (x10, xm0, x01) for t in (p, to_core(p))]
    whole = tuple((i, i, 0, 0, 768) for i in range(6))
    acc = logits_part(near, whole, (1, 2, 3), idx, w, acc)[0]
    f1, f2, f3, acc = lax.optimization_barrier((f1, f2, f3, acc))
    g1 = to_y(f3[:h], -1)
    g2 = to_z(f2[h:])
    mid = [t for p in (f1, f2, f3) for t in (p, to_core(p))]
    mid_copies = []
    for c in range(2):
        mid_copies += [
            (0 + c, 0 + c, 0, 0, h),
            (2 + c, 0 + c, h, h, h),
            (4 + c, 2 + c, 0, 0, h),
            (0 + c, 2 + c, h, h, h),
            (4 + c, 4 + c, h, 0, h),
            (2 + c, 4 + c, 0, h, h),
        ]
    acc, w21 = logits_part(mid, tuple(mid_copies), (4, 5, 6), idx, w, acc, 7)
    g1, g2, acc = lax.optimization_barrier((g1, g2, acc))
    last = [t for p in (g1, g2) for t in (p, to_core(p))]
    last_copies = tuple((2 * i + c, c, 0, h * i, h) for i in range(2) for c in range(2))
    query_mask, passage_mask, positive = lax.optimization_barrier((query_mask, passage_mask, positive, x10))[:3]
    lens = jnp.concatenate([jnp.sum(query_mask > 0, axis=1), jnp.sum(passage_mask > 0, axis=1)]).astype(jnp.int32)
    expo, stats, pooled = logits_pool(last, last_copies, lens, w21, acc, seqs)

    pa = jnp.concatenate([pooled] + [to_x(pooled, -k) for k in (1, 2, 3)], axis=0)
    pb = to_zhi(pa)
    parts = lax.all_to_all(gram(pa, pb, 16), "vocab", 0, 0)

    seq = idx[16:]
    target = positive[seq]
    picked = (target[:, None] == seq[None, :]).astype(F32)

    dl, loss, m21, s21, ahead = first_grad(7, 4, idx, parts, pa, pb, stats, picked, expo, w, seqs, positive.shape[0])
    t21 = (m21 + to_core(s21)).astype(BF)
    def rows(x, i):
        return x[768 * i : 768 * (i + 1)]

    r1, r2 = to_y(t21[:h], 1), to_z(t21[h:])
    mb, sb = grad_part(4, 3, idx, after(dl, t21), w, ahead)
    sb = to_core(sb)
    (mb,) = add_arrived((mb,), (r1, r2), ((0, 0, 0, 768, h), (0, 1, 0, h, h)))
    t20, t11, tm1 = ((rows(mb, i) + rows(sb, i)).astype(BF) for i in range(3))
    c1 = jnp.concatenate([t20[:h], t11[h:]], axis=0)
    c2 = jnp.concatenate([tm1[h:], t20[h:]], axis=0)
    c3 = jnp.concatenate([t11[:h], tm1[:h]], axis=0)
    c1, c2, c3, dl = lax.optimization_barrier((c1, c2, c3, dl))
    u1, u2, u3 = to_y(c1, 1), to_y(c2, -1), to_z(c3)
    mc, sc = grad_part(1, 3, idx, dl, w)
    sc = to_core(sc)
    (mc,) = add_arrived(
        (mc,),
        (u1, u2, u3),
        (
            (0, 0, 0, 0, h),
            (0, 2, 0, 0, h),
            (0, 2, h, 768, h),
            (0, 1, h, 768 + h, h),
            (0, 0, h, 1536 + h, h),
            (0, 1, 0, 1536 + h, h),
        ),
    )
    t10, tm0, t01 = ((rows(mc, i) + rows(sc, i)).astype(BF) for i in range(3))
    t10, tm0, t01, dl = lax.optimization_barrier((t10, tm0, t01, dl))
    v1, v2, v3 = to_y(t10, 1), to_y(tm0, -1), to_z(t01)
    md, sd = grad_part(0, 1, idx, dl, w)
    (md,) = add_arrived((md,), (v1, v2, v3), tuple((0, i, 0, 0, 768) for i in range(3)))
    out_q, out_p = add_last(md, (to_core(sd),), split)
    return (
        out_q.reshape(q_count, q_len, width),
        out_p.reshape(p_count, p_len, width),
        loss[:q_count, 0],
    )


def solution(mesh):
    return jax.shard_map(
        on_device,
        mesh=mesh,
        in_specs=(
            P("dp", None, "vocab"),
            P("dp", None, "vocab"),
            P(None, "vocab"),
            P("dp", None),
            P("dp", None),
            P(),
        ),
        out_specs=(P("dp", None, "vocab"), P("dp", None, "vocab"), P("dp")),
        check_vma=False,
    )
```

```python
import functools

import jax
import jax.numpy as jnp
import numpy as np
from jax import lax
from jax.experimental import pallas as pl
from jax.experimental.pallas import tpu as pltpu
from jax.sharding import PartitionSpec as P

SHARP = 0.2
DIV = 16.0
LOSS_SCALE = 65536.0
BF = jnp.bfloat16
F32 = jnp.float32
MIB = 1024 * 1024
BLK = 256
HBM_SPEC = pl.BlockSpec(memory_space=pltpu.HBM)


def y_perm(k):
    return [(z * 8 + y * 2 + c, z * 8 + ((y + k) % 4) * 2 + c) for z in range(2) for y in range(4) for c in range(2)]


Z_SWAP = [(v, v ^ 8) for v in range(16)]
CORE_SWAP = [(v, v ^ 1) for v in range(16)]


def to_y(x, k):
    return lax.ppermute(x, "vocab", y_perm(k % 4))


def to_z(x):
    return lax.ppermute(x, "vocab", Z_SWAP)


def to_core(x):
    return lax.ppermute(x, "vocab", CORE_SWAP)


def to_x(x, k):
    return lax.ppermute(x, "dp", [(g, ((g // 2 + k) % 4) * 2 + g % 2) for g in range(8)])


def to_zhi(x):
    return lax.ppermute(x, "dp", [(g, g ^ 1) for g in range(8)])


PLACES = ((0, 0), (1, 0), (-1, 0), (0, 1), (2, 0), (1, 1), (-1, 1), (2, 1))


def place_table():
    rows = []
    for g in range(8):
        gx, gz = g // 2, g % 2
        seqs = [(((gx + i % 4) % 4) * 2 + (gz + i // 4) % 2) * 2 + k for i in range(8) for k in range(2)]
        for v in range(16):
            z, y, core = v // 8, (v // 2) % 4, v % 2
            rows.append([((z + dz) % 2) * 4 + (y + dy) % 4 for dy, dz in PLACES] + [core] * 8 + seqs)
    return np.array(rows, np.int32)


def matmul_cost(m, k, n):
    return pl.CostEstimate(flops=2 * m * k * n, bytes_accessed=2 * k * n, transcendentals=0)


def load_operands(copies, places, bn, steps, idx, xrefs, w, xs, ws, xsem, wsem):
    j = pl.program_id(0)
    nk = 2 * len(places)

    def x_copy(i):
        a, k, src, dst, n = copies[i]
        return pltpu.make_async_copy(
            xrefs[a].at[pl.ds(src, n), :], xs.at[pl.ds(dst, n), pl.ds(k * BLK, BLK)], xsem.at[i]
        )

    def w_copy(step, slot, k):
        core = idx[8]
        side = core if k % 2 == 0 else 1 - core
        row = pl.multiple_of((idx[places[k // 2]] * 2 + side) * BLK, BLK)
        col = pl.multiple_of(step * bn, bn)
        return pltpu.make_async_copy(
            w.at[pl.ds(row, BLK), pl.ds(col, bn)], ws.at[slot, pl.ds(k * BLK, BLK), :], wsem.at[slot, k]
        )

    slot = lax.rem(j, 2)

    @pl.when(j == 0)
    def _():
        for k in range(nk):
            w_copy(0, 0, k).start()
        for i in range(len(copies)):
            x_copy(i).start()

    @pl.when(j == 0)
    def _():
        for i in range(len(copies)):
            x_copy(i).wait()

    for k in range(nk):
        w_copy(j, slot, k).wait()

    @pl.when(j + 1 < steps)
    def _():
        for k in range(nk):
            w_copy(j + 1, 1 - slot, k).start()

    return slot


def columns_of(bn):
    return pl.ds(pl.multiple_of(pl.program_id(0) * bn, bn), bn)


def logits_kernel(copies, places, nx, bn, steps, has_acc, following, idx, *refs):
    xrefs = refs[:nx]
    w = refs[nx]
    pos = nx + 1
    acc = None
    if has_acc:
        acc = refs[pos]
        pos += 1
    out = refs[pos]
    if following is not None:
        ahead, asem = refs[pos + 1], refs[-1]
        refs = refs[:-1]
        ahead_copies = [
            pltpu.make_async_copy(
                w.at[pl.ds(pl.multiple_of((idx[following] * 2 + side) * BLK, BLK), BLK), :],
                ahead.at[pl.ds(k * BLK, BLK), :],
                asem.at[k],
            )
            for k, side in enumerate((idx[8], 1 - idx[8]))
        ]
    xs, ws, xsem, wsem = refs[-4:]
    slot = load_operands(copies, places, bn, steps, idx, xrefs, w, xs, ws, xsem, wsem)
    if following is not None:

        @pl.when(pl.program_id(0) == 0)
        def _():
            for c in ahead_copies:
                c.start()

        @pl.when(pl.program_id(0) == steps - 1)
        def _():
            for c in ahead_copies:
                c.wait()

    res = jnp.dot(xs[...], ws[slot], preferred_element_type=F32)
    cols = columns_of(bn)
    if has_acc:
        res = res + acc[:, cols]
    out[:, cols] = res


def logits_part(arrays, copies, places, idx, w, acc, following=None):
    rows = 768
    cols = w.shape[1]
    nk = 2 * len(places)
    bn = 512
    steps = cols // bn
    any_spec = pl.BlockSpec(memory_space=pl.ANY)
    vm = pl.BlockSpec(memory_space=pltpu.VMEM)
    ins = list(arrays) + [w] + ([acc] if acc is not None else [])
    return pl.pallas_call(
        functools.partial(logits_kernel, copies, places, len(arrays), bn, steps, acc is not None, following),
        grid_spec=pltpu.PrefetchScalarGridSpec(
            num_scalar_prefetch=1,
            grid=(steps,),
            in_specs=[any_spec] * len(arrays) + [HBM_SPEC] + ([vm] if acc is not None else []),
            out_specs=[vm] * (1 if following is None else 2),
            scratch_shapes=[
                pltpu.VMEM((rows, nk * BLK), BF),
                pltpu.VMEM((2, nk * BLK, bn), BF),
                pltpu.SemaphoreType.DMA((len(copies),)),
                pltpu.SemaphoreType.DMA((2, nk)),
            ]
            + ([] if following is None else [pltpu.SemaphoreType.DMA((2,))]),
        ),
        out_shape=[jax.ShapeDtypeStruct((rows, cols), F32)]
        + ([] if following is None else [jax.ShapeDtypeStruct((2 * BLK, cols), BF)]),
        input_output_aliases={len(arrays) + 2: 0} if acc is not None else {},
        compiler_params=pltpu.CompilerParams(vmem_limit_bytes=(14 if nk > 2 else 12) * MIB),
        name="logits_part",
    )(idx, *ins)


def pool_kernel(copies, nx, bn, seqs, lens, *refs):
    xrefs = refs[:nx]
    ws, acc, expo, stats, pooled, xs, es, xsem, esem = refs[nx:]
    steps = ws.shape[1] // bn
    loads = []
    for i, (a, k, src, dst, n) in enumerate(copies):
        loads.append(
            pltpu.make_async_copy(
                xrefs[a].at[pl.ds(src, n), :], xs.at[pl.ds(dst, n), pl.ds(k * BLK, BLK)], xsem.at[i]
            )
        )
    for c in loads:
        c.start()
    for c in loads:
        c.wait()
    outs = []
    for j in range(steps):
        cols = pl.ds(j * bn, bn)
        logits = jnp.dot(xs[...], ws[:, cols], preferred_element_type=F32) + acc[:, cols]
        smooth, sums = [], []
        for s, (start, n) in enumerate(seqs):
            live = lax.broadcasted_iota(jnp.int32, (n, 1), 0) < lens[s]
            part = jnp.where(live, logits[start : start + n], -1e30)
            top = jnp.max(part, axis=0, keepdims=True)
            e = jnp.exp((part - top) * (1.0 / SHARP))
            total = jnp.sum(e, axis=0, keepdims=True)
            es[pl.ds(start, n), cols] = e.astype(BF)
            smooth.append(top + SHARP * jnp.log(total))
            sums.append(total)
        both = jnp.concatenate(smooth + sums, axis=0)
        stats[:, cols] = both
        pooled[:, cols] = jnp.log1p(jnp.maximum(both[:4], 0.0))
        out = pltpu.make_async_copy(es.at[:, cols], expo.at[:, cols], esem.at[j])
        out.start()
        outs.append(out)
    for out in outs:
        out.wait()


def logits_pool(arrays, copies, lens, w, acc, seqs):
    rows = 768
    cols = w.shape[1]
    bn = 512
    any_spec = pl.BlockSpec(memory_space=pl.ANY)
    vm = pl.BlockSpec(memory_space=pltpu.VMEM)
    sm = pl.BlockSpec(memory_space=pltpu.SMEM)
    return pl.pallas_call(
        functools.partial(pool_kernel, copies, len(arrays), bn, seqs),
        in_specs=[sm] + [any_spec] * len(arrays) + [vm, vm],
        out_specs=[HBM_SPEC, vm, vm],
        scratch_shapes=[
            pltpu.VMEM((rows, 2 * BLK), BF),
            pltpu.VMEM((rows, cols), BF),
            pltpu.SemaphoreType.DMA((len(copies),)),
            pltpu.SemaphoreType.DMA((cols // bn,)),
        ],
        out_shape=[
            pltpu.HBM((rows, cols), BF),
            jax.ShapeDtypeStruct((8, cols), F32),
            jax.ShapeDtypeStruct((4, cols), F32),
        ],
        compiler_params=pltpu.CompilerParams(vmem_limit_bytes=16 * MIB),
        name="logits_pool",
    )(lens, *arrays, w, acc)


def exact_dot(a, b, dims):
    return lax.dot_general(a, b, (dims, ((), ())), precision=lax.Precision.HIGHEST, preferred_element_type=F32)


def split_kinds(a, b):
    every = jnp.concatenate([a, b], axis=0)
    q = jnp.concatenate([every[i : i + 2] for i in range(0, every.shape[0], 4)], axis=0)
    p = jnp.concatenate([every[i + 2 : i + 4] for i in range(0, every.shape[0], 4)], axis=0)
    return q, p


def gram_kernel(a, b, out):
    q, p = split_kinds(a[...], b[...])
    res = exact_dot(q, p, ((1,), (1,)))
    res = jnp.concatenate([res[:8], res[8:], jnp.zeros((8, 96), F32)], axis=1)
    for i in range(out.shape[0]):
        out[i] = res


def gram(a, b, copies):
    return pl.pallas_call(
        gram_kernel,
        out_shape=jax.ShapeDtypeStruct((copies, 8, 128), F32),
        compiler_params=pltpu.CompilerParams(vmem_limit_bytes=4 * MIB),
        name="gram",
    )(a, b)


def nt_dot(a, b):
    return lax.dot_general(a, b, (((1,), (1,)), ((), ())), preferred_element_type=F32)


def store_halves(core, res, mine, sib):
    left, right = res[:, :BLK], res[:, BLK:]

    @pl.when(core == 0)
    def _():
        mine[...] = left
        sib[...] = right.astype(BF)

    @pl.when(core != 0)
    def _():
        mine[...] = right
        sib[...] = left.astype(BF)


def first_grad_kernel(
    seqs, place, following, total_queries, idx, parts, pa, pb, stats, picked, expo, w, dl, loss, mine, sib, ahead, es, ws, esem, wsem
):
    e_copies = [
        pltpu.make_async_copy(expo.at[pl.ds(start, n), :], es.at[pl.ds(start, n), :], esem.at[s])
        for s, (start, n) in enumerate(seqs)
    ]
    row0 = pl.multiple_of(idx[place] * (2 * BLK), 2 * BLK)
    w_copy = pltpu.make_async_copy(w.at[pl.ds(row0, 2 * BLK), :], ws, wsem.at[0])
    row1 = pl.multiple_of(idx[following] * (2 * BLK), 2 * BLK)
    ahead_copy = pltpu.make_async_copy(w.at[pl.ds(row1, 2 * BLK), :], ahead, wsem.at[1])
    for c in e_copies:
        c.start()
    w_copy.start()
    ahead_copy.start()
    scores = parts[0]
    for i in range(1, parts.shape[0]):
        scores = scores + parts[i]
    scores = jnp.concatenate([scores[:, :16], scores[:, 16:32]], axis=0) / DIV
    top = jnp.max(scores, axis=1, keepdims=True)
    lse = top + jnp.log(jnp.sum(jnp.exp(scores - top), axis=1, keepdims=True))
    pick = picked[...]
    losses = lse - jnp.sum(scores * pick, axis=1, keepdims=True)
    loss[...] = jnp.broadcast_to(losses[:8], loss.shape)
    dscores = (jnp.exp(scores - lse) - pick) * (LOSS_SCALE / total_queries)
    q, p = split_kinds(pa[...], pb[...])
    dq = exact_dot(dscores[:8], p, ((1,), (0,)))
    dp = exact_dot(dscores.T[:8], q, ((1,), (0,)))
    dpooled = jnp.concatenate([dq[:2], dp[:2]], axis=0) / DIV
    smooth = stats[0:4, :]
    gate = jnp.where(smooth > 0, 1.0 / (1.0 + jnp.maximum(smooth, 0.0)), 0.0)
    g = dpooled * gate / stats[4:8, :]
    for s, (start, n) in enumerate(seqs):
        e_copies[s].wait()
        dl[pl.ds(start, n), :] = (es[pl.ds(start, n), :].astype(F32) * g[s : s + 1, :]).astype(BF)
    w_copy.wait()
    store_halves(idx[8], nt_dot(dl[...], ws[...]), mine, sib)
    ahead_copy.wait()


def first_grad(place, following, idx, parts, pa, pb, stats, picked, expo, w, seqs, total_queries):
    rows, cols = expo.shape
    vm = pl.BlockSpec(memory_space=pltpu.VMEM)
    return pl.pallas_call(
        functools.partial(first_grad_kernel, seqs, place, following, total_queries),
        in_specs=[pl.BlockSpec(memory_space=pltpu.SMEM)] + [vm] * 5 + [HBM_SPEC] * 2,
        out_specs=[vm] * 5,
        scratch_shapes=[
            pltpu.VMEM((rows, cols), BF),
            pltpu.VMEM((2 * BLK, cols), BF),
            pltpu.SemaphoreType.DMA((len(seqs),)),
            pltpu.SemaphoreType.DMA((2,)),
        ],
        out_shape=[
            jax.ShapeDtypeStruct((rows, cols), BF),
            jax.ShapeDtypeStruct((8, 128), F32),
            jax.ShapeDtypeStruct((rows, BLK), F32),
            jax.ShapeDtypeStruct((rows, BLK), BF),
            jax.ShapeDtypeStruct((2 * BLK, cols), BF),
        ],
        compiler_params=pltpu.CompilerParams(vmem_limit_bytes=18 * MIB),
        name="first_grad",
    )(idx, parts, pa, pb, stats, picked, pltpu.with_memory_space_constraint(expo, pltpu.HBM), w)


def grad_kernel(first, n, has_ahead, following, idx, dl, w, *refs):
    ahead = refs[0] if has_ahead else None
    mine, sib = refs[has_ahead : has_ahead + 2]
    ws, wsem = refs[-2:]

    def w_copy(step):
        row = pl.multiple_of(idx[first + step] * (2 * BLK), 2 * BLK)
        return pltpu.make_async_copy(w.at[pl.ds(row, 2 * BLK), :], ws.at[step - has_ahead], wsem.at[step - has_ahead])

    for i in range(has_ahead, n):
        w_copy(i).start()
    if following is not None:
        row = pl.multiple_of(idx[following] * (2 * BLK), 2 * BLK)
        later = pltpu.make_async_copy(w.at[pl.ds(row, 2 * BLK), :], refs[has_ahead + 2], wsem.at[n - has_ahead])
        later.start()
    rows = dl.shape[0]
    for i in range(n):
        here = pl.ds(i * rows, rows)
        if i < has_ahead:
            block = ahead[...]
        else:
            w_copy(i).wait()
            block = ws[i - has_ahead]
        store_halves(idx[8], nt_dot(dl[...], block), mine.at[here], sib.at[here])
    if following is not None:
        later.wait()


def grad_part(first, n, idx, dl, w, ahead=None, following=None):
    rows, cols = dl.shape
    vm = pl.BlockSpec(memory_space=pltpu.VMEM)
    has = 0 if ahead is None else 1
    more = 0 if following is None else 1
    return pl.pallas_call(
        functools.partial(grad_kernel, first, n, has, following),
        in_specs=[pl.BlockSpec(memory_space=pltpu.SMEM), vm, HBM_SPEC] + [vm] * has,
        out_specs=[vm] * (2 + more),
        scratch_shapes=[
            pltpu.VMEM((max(n - has, 1), 2 * BLK, cols), BF),
            pltpu.SemaphoreType.DMA((max(n - has + more, 1),)),
        ],
        out_shape=[jax.ShapeDtypeStruct((n * rows, BLK), F32), jax.ShapeDtypeStruct((n * rows, BLK), BF)]
        + [jax.ShapeDtypeStruct((2 * BLK, cols), BF)] * more,
        compiler_params=pltpu.CompilerParams(vmem_limit_bytes=16 * MIB),
        name="grad_part",
    )(idx, dl, w, *([ahead] if has else []))


def add_kernel(spec, n_mine, *refs):
    outs = refs[len(refs) - n_mine :]
    for i in range(n_mine):
        outs[i][...] = refs[i][...]
    for i, a, src, dst, n in spec:
        outs[i][pl.ds(dst, n), :] = outs[i][pl.ds(dst, n), :] + refs[n_mine + a][pl.ds(src, n), :].astype(F32)


def add_arrived(mine, arrived, spec):
    return pl.pallas_call(
        functools.partial(add_kernel, spec, len(mine)),
        out_shape=[jax.ShapeDtypeStruct(m.shape, F32) for m in mine],
        compiler_params=pltpu.CompilerParams(vmem_limit_bytes=12 * MIB),
        name="add_arrived",
        cost_estimate=matmul_cost(4096, 2048, 2048),
    )(*mine, *arrived)


def add_last_kernel(split, *refs):
    parts, (out_q, out_p) = refs[:-2], refs[-2:]
    res = parts[0][...]
    for p in parts[1:]:
        res = res + p[...].astype(F32)
    res = res.astype(BF)
    out_q[...] = res[:split]
    out_p[...] = res[split:]


def add_last(mine, others, split):
    rows, cols = mine.shape
    return pl.pallas_call(
        functools.partial(add_last_kernel, split),
        out_shape=[jax.ShapeDtypeStruct((split, cols), BF), jax.ShapeDtypeStruct((rows - split, cols), BF)],
        compiler_params=pltpu.CompilerParams(vmem_limit_bytes=12 * MIB),
        name="add_last",
    )(mine, *others)


def after(x, *others):
    return lax.optimization_barrier((x,) + others)[0]


def on_device(query_hidden, passage_hidden, head_weight, query_mask, passage_mask, positive):
    q_count, q_len, width = query_hidden.shape
    p_count, p_len, _ = passage_hidden.shape
    w = pltpu.with_memory_space_constraint(head_weight, pltpu.HBM)
    split = q_count * q_len
    seqs = tuple((i * q_len, q_len) for i in range(q_count)) + tuple(
        (split + i * p_len, p_len) for i in range(p_count)
    )
    own = jnp.concatenate([query_hidden.reshape(split, width), passage_hidden.reshape(p_count * p_len, width)], axis=0)
    me = lax.axis_index(("dp", "vocab"))
    idx = lax.dynamic_index_in_dim(jnp.asarray(place_table()), me, 0, keepdims=False)
    at = {p: i for i, p in enumerate(PLACES)}
    h = 384

    x10, xm0, x01 = to_y(own, -1), to_y(own, 1), to_z(own)
    own_s = to_core(own)
    acc = logits_part([own, own_s], ((0, 0, 0, 0, 768), (1, 1, 0, 0, 768)), (0,), idx, w, None)[0]
    x10, xm0, x01, acc = lax.optimization_barrier((x10, xm0, x01, acc))
    f1 = to_y(jnp.concatenate([x10[:h], x01[h:]], axis=0), -1)
    f2 = to_y(jnp.concatenate([x01[h:], xm0[h:]], axis=0), 1)
    f3 = to_z(jnp.concatenate([x10[:h], xm0[:h]], axis=0))
    near = [t for p in (x10, xm0, x01) for t in (p, to_core(p))]
    whole = tuple((i, i, 0, 0, 768) for i in range(6))
    acc = logits_part(near, whole, (1, 2, 3), idx, w, acc)[0]
    f1, f2, f3, acc = lax.optimization_barrier((f1, f2, f3, acc))
    g1 = to_y(f3[:h], -1)
    g2 = to_z(f2[h:])
    mid = [t for p in (f1, f2, f3) for t in (p, to_core(p))]
    mid_copies = []
    for c in range(2):
        mid_copies += [
            (0 + c, 0 + c, 0, 0, h),
            (2 + c, 0 + c, h, h, h),
            (4 + c, 2 + c, 0, 0, h),
            (0 + c, 2 + c, h, h, h),
            (4 + c, 4 + c, h, 0, h),
            (2 + c, 4 + c, 0, h, h),
        ]
    acc, w21 = logits_part(mid, tuple(mid_copies), (4, 5, 6), idx, w, acc, 7)
    g1, g2, acc = lax.optimization_barrier((g1, g2, acc))
    last = [t for p in (g1, g2) for t in (p, to_core(p))]
    last_copies = tuple((2 * i + c, c, 0, h * i, h) for i in range(2) for c in range(2))
    query_mask, passage_mask, positive = lax.optimization_barrier((query_mask, passage_mask, positive, x10))[:3]
    lens = jnp.concatenate([jnp.sum(query_mask > 0, axis=1), jnp.sum(passage_mask > 0, axis=1)]).astype(jnp.int32)
    expo, stats, pooled = logits_pool(last, last_copies, lens, w21, acc, seqs)

    pa = jnp.concatenate([pooled] + [to_x(pooled, -k) for k in (1, 2, 3)], axis=0)
    pb = to_zhi(pa)
    parts = lax.all_to_all(gram(pa, pb, 16), "vocab", 0, 0)

    seq = idx[16:]
    target = positive[seq]
    picked = (target[:, None] == seq[None, :]).astype(F32)

    dl, loss, m21, s21, ahead = first_grad(7, 4, idx, parts, pa, pb, stats, picked, expo, w, seqs, positive.shape[0])
    t21 = (m21 + to_core(s21)).astype(BF)
    def rows(x, i):
        return x[768 * i : 768 * (i + 1)]

    r1, r2 = to_y(t21[:h], 1), to_z(t21[h:])
    mb, sb, ahead = grad_part(4, 3, idx, after(dl, t21), w, ahead, 1)
    sb = to_core(sb)
    (mb,) = add_arrived((mb,), (r1, r2), ((0, 0, 0, 768, h), (0, 1, 0, h, h)))
    t20, t11, tm1 = ((rows(mb, i) + rows(sb, i)).astype(BF) for i in range(3))
    c1 = jnp.concatenate([t20[:h], t11[h:]], axis=0)
    c2 = jnp.concatenate([tm1[h:], t20[h:]], axis=0)
    c3 = jnp.concatenate([t11[:h], tm1[:h]], axis=0)
    c1, c2, c3, dl = lax.optimization_barrier((c1, c2, c3, dl))
    u1, u2, u3 = to_y(c1, 1), to_y(c2, -1), to_z(c3)
    mc, sc, ahead = grad_part(1, 3, idx, dl, w, ahead, 0)
    sc = to_core(sc)
    (mc,) = add_arrived(
        (mc,),
        (u1, u2, u3),
        (
            (0, 0, 0, 0, h),
            (0, 2, 0, 0, h),
            (0, 2, h, 768, h),
            (0, 1, h, 768 + h, h),
            (0, 0, h, 1536 + h, h),
            (0, 1, 0, 1536 + h, h),
        ),
    )
    t10, tm0, t01 = ((rows(mc, i) + rows(sc, i)).astype(BF) for i in range(3))
    t10, tm0, t01, dl = lax.optimization_barrier((t10, tm0, t01, dl))
    v1, v2, v3 = to_y(t10, 1), to_y(tm0, -1), to_z(t01)
    md, sd = grad_part(0, 1, idx, dl, w, ahead)
    (md,) = add_arrived((md,), (v1, v2, v3), tuple((0, i, 0, 0, 768) for i in range(3)))
    out_q, out_p = add_last(md, (to_core(sd),), split)
    return (
        out_q.reshape(q_count, q_len, width),
        out_p.reshape(p_count, p_len, width),
        loss[:q_count, 0],
    )


def solution(mesh):
    return jax.shard_map(
        on_device,
        mesh=mesh,
        in_specs=(
            P("dp", None, "vocab"),
            P("dp", None, "vocab"),
            P(None, "vocab"),
            P("dp", None),
            P("dp", None),
            P(),
        ),
        out_specs=(P("dp", None, "vocab"), P("dp", None, "vocab"), P("dp")),
        check_vma=False,
    )
```
